32 devices in a mesh: group: 2 (over x), req: 4 (over z), tp: 4 (over y, core).
Axes of the slice: x: 2, y: 2, z: 4, core: 2. Of those that a mesh axis runs over, the one named last changes fastest.
Arguments:
- tokens: bfloat16 [1024, 4096], P(('group', 'req'), 'tp'), parts along dimension 0, may hold values from -400 to 400
- norm_gain: bfloat16 [4096], P('tp'), may hold values from 0.099609375 to 1.8984375
- query_weight: bfloat16 [4096, 4096], P(None, 'tp'), may hold values from -0.09375 to 0.09375
- keyval_weight: bfloat16 [4096, 1024], P(None, 'tp'), may hold values from -0.09375 to 0.09375
- output_weight: bfloat16 [4096, 4096], P('tp'), may hold values from -0.5 to 0.5
- projection_down_weight: bfloat16 [256, 4096, 64], P(('group', 'req'), 'tp'), parts along dimension 0, may hold values from -0.09375 to 0.09375
- query_up_weight: bfloat16 [256, 64, 4096], P(('group', 'req'), None, 'tp'), parts along dimension 0, may hold values from -0.75 to 0.75
- keyval_up_weight: bfloat16 [256, 64, 1024], P(('group', 'req'), None, 'tp'), parts along dimension 0, may hold values from -0.75 to 0.75
- output_down_weight: bfloat16 [256, 4096, 64], P(('group', 'req'), 'tp'), parts along dimension 0, may hold values from -0.375 to 0.375
- output_up_weight: bfloat16 [256, 64, 4096], P(('group', 'req'), None, 'tp'), parts along dimension 0, may hold values from -0.75 to 0.75
- adapter_ids: int32 [1024], P('group'), parts along dimension 0, may hold values from 0 to 127, as said below
- adapter_slot: int32 [256], P('group'), parts along dimension 0, may hold values from 0 to 127, as said below
- kv_cache: bfloat16 [1024, 192, 1024], P(('group', 'req', 'tp')), parts along dimension 0, may hold values from -600 to 600
- cache_len: int32 [1024], P(('group', 'req', 'tp')), parts along dimension 0, may hold values from 1 to 192, 49152 in all
Outputs:
- layer_out: bfloat16 [1024, 4096], P(('group', 'req'), 'tp'), parts along dimension 0
The draws below stay inside these ranges and needn't reach their ends.
There are 2 independent parts, one for each index of `group`. The reference program is written for one: setup_inputs(seed, part) draws one part's arguments, and reference() takes and returns one part's arrays. A program takes and returns all parts, laid end to end along the dimension named above; an argument that names none is the same for every part. Nothing has to cross between parts.
Inputs may be any that keep to these rules, and one draw needn't show every extreme that they name: Each of 0 to 127 once: adapter a lies at row adapter_slot[a] of the adapter arrays, held by index adapter_slot[a] // 32 of req. `adapter_ids`: of the 128 requests of one index of req, at most 64 use adapters held by any one index of req, and these name at most 2 distinct adapters; in every draw one holding index is used by exactly 64 requests naming exactly 2 adapters of every index of req.
All inputs are finite; a program needn't handle non-finite values. No bound on the sum of `cache_len` on one device may be relied on, other than what follows from the above.
Results may differ from the reference program's by a relative error of at most 0.014.
The reference program's roundings to bfloat16 on the way count: a program that leaves them out, or rounds other values in their place, can miss the bound.
Values may be sent and summed in bfloat16 or wider, within the bound.
A program may use at most 192 MiB of HBM per device.

```python
import math
import jax
import jax.numpy as jnp
import numpy as np
from jax import lax

D = 4096
QH = 32
KVH = 4
HD = 128
RANK = 64
ADP_DEV = 32
FETCH_OWN = 2
REQ_DEV = 128
CTX = 192
ADAPTERS = 128
REQS = 512
N_REQ = 4
N_TP = 4


def adapter_plan(key):
    slot_of = jax.random.permutation(jax.random.fold_in(key, 101), ADAPTERS).astype(jnp.int32)
    stored_at = jnp.argsort(slot_of).astype(jnp.int32)
    busiest = jax.random.randint(jax.random.fold_in(key, 102), (), 0, N_REQ)
    capacity = 2 * REQ_DEV // N_REQ
    marker = jnp.arange(REQ_DEV, dtype=jnp.int32)[None, :]
    rotation = jax.random.randint(jax.random.fold_in(key, 103), (N_REQ, 1), 0, N_REQ - 1)
    others = (marker - capacity + rotation) % (N_REQ - 1)
    others = others + (others >= busiest).astype(jnp.int32)
    holder = jnp.where(marker < capacity, busiest, others)
    picked = jax.random.randint(jax.random.fold_in(key, 104), (N_REQ, REQ_DEV), 0, FETCH_OWN)
    picked = jnp.where(marker < capacity, marker % FETCH_OWN, picked)
    subkeys = jax.random.split(jax.random.fold_in(key, 105), N_REQ * N_REQ)
    offered = jax.vmap(lambda subkey: jax.random.permutation(subkey, ADP_DEV)[:FETCH_OWN])(subkeys)
    offered = offered.reshape(N_REQ, N_REQ, FETCH_OWN).astype(jnp.int32)
    sources = jnp.arange(N_REQ, dtype=jnp.int32)[:, None]
    local_index = offered[sources, holder, picked]
    adapter = stored_at[holder * ADP_DEV + local_index]
    positions = jax.vmap(lambda subkey: jax.random.permutation(subkey, REQ_DEV))(jax.random.split(jax.random.fold_in(key, 106), N_REQ))
    placed = jnp.zeros((N_REQ, REQ_DEV), jnp.int32).at[sources, positions].set(adapter)
    return (slot_of, placed.reshape(REQS))


def draw_adapter_slot(key, part):
    slot_of, placed = adapter_plan(key)
    return slot_of


def draw_adapter_ids(key, part):
    slot_of, placed = adapter_plan(key)
    return placed


def draw_tokens(key, part):
    key = jax.random.fold_in(key, 1)
    row_scale = jnp.exp(jax.random.uniform(jax.random.fold_in(key, 1), (REQS, 1), minval=0.0, maxval=2.31))
    column_scale = jnp.exp(jax.random.uniform(jax.random.fold_in(key, 2), (1, D), minval=0.0, maxval=2.31))
    values = jax.random.normal(jax.random.fold_in(key, 3), (REQS, D)) * row_scale * column_scale
    return jnp.clip(values, -400.0, 400.0).astype(jnp.bfloat16)


def draw_kv_cache(key, part):
    key = jax.random.fold_in(key, 2)
    row_width = 2 * KVH * HD
    return jax.random.normal(jax.random.fold_in(key, 1), (REQS, CTX, row_width)).astype(jnp.bfloat16)


def with_spikes(result, own_key, source, target, shards_of, factor):
    owner, partner = [(jnp.arange(result.shape[axis_at]) // (result.shape[axis_at] // shards_of)).reshape([-1 if axis == axis_at else 1 for axis in range(result.ndim)]) for axis_at in (source, target)]
    chosen = jax.random.permutation(own_key, shards_of)[partner]
    strong = (owner == chosen) | (owner == (partner + shards_of // 2) % shards_of)
    return jnp.where(strong, factor * result, result)


def level_of(rng, dims, cuts, low, top_value):
    level, own = 1.0, jax.random.fold_in(rng, 6)
    for dim, blocks in cuts:
        heights = jnp.exp(jax.random.uniform(jax.random.fold_in(own, dim), (blocks,), jnp.float32, low / len(cuts), top_value / len(cuts)))
        level = level * jnp.repeat(heights, dims[dim] // blocks).reshape([-1 if axis == dim else 1 for axis in range(len(dims))])
    return level


def profile(count, total, reach, slope):
    loads = [(1 << 20) // math.isqrt(grade ** slope) + 1 for grade in range(2, count + 1)]
    spare, given = total - reach - (count - 1), [1] * (count - 1)
    while spare > 0:
        free = [i for i in range(count - 1) if given[i] < reach]
        mass, remaining = sum([loads[i] for i in free]), spare
        for i in free:
            extra = min(reach - given[i], max(1, remaining * loads[i] // mass), spare)
            given[i] = given[i] + extra
            spare = spare - extra
    return np.array([reach] + given)


def uneven_parts(stream_key, amount, total, bound, skew):
    if amount == 2:
        one = jax.random.randint(stream_key, (), max(1, total - bound), min(bound, total - 1) + 1)
        return jnp.stack([one, total - one])
    sizes = jnp.asarray(profile(amount, total, bound, skew), jnp.int32)
    couples = (amount - 1) // 2
    donor, taker = sizes[1:1 + 2 * couples:2], sizes[2:2 + 2 * couples:2]
    margin = jnp.minimum(donor - 1, bound - taker)
    passed = jax.random.randint(jax.random.fold_in(stream_key, 1), (couples,), 0, 1 << 20) % (margin + 1)
    sizes = sizes.at[1:1 + 2 * couples:2].set(donor - passed).at[2:2 + 2 * couples:2].set(taker + passed)
    return sizes[jax.random.permutation(jax.random.fold_in(stream_key, 2), amount)]


def centred(rng, dims, spread, limit, shards=(), kind=jnp.bfloat16):
    array = spread * jax.random.normal(rng, dims, jnp.float32)
    if shards:
        array = array * level_of(rng, dims, shards, -0.22, 0.18)
    return jnp.clip(array, -limit, limit).astype(kind)


def noise_with(stream_key, extent, deviation, reach, cuts, heavy, kind=jnp.bfloat16):
    result = deviation * jax.random.normal(stream_key, extent, jnp.float32)
    if cuts:
        result = result * level_of(stream_key, extent, cuts, -0.22, 0.18)
    return jnp.clip(with_spikes(result, jax.random.fold_in(stream_key, 3), *heavy), -reach, reach).astype(kind)


def setup_inputs(seed: int = 0, part: int = 0) -> dict:
    keys = jax.random.split(jax.random.key(seed), 15)
    part_keys = jax.random.split(jax.random.fold_in(keys[14], part), 15)
    tokens = draw_tokens(jax.random.fold_in(jax.random.fold_in(keys[14], part), 71), part)
    norm_gain = jnp.clip(1.0 + 0.18 * jax.random.normal(keys[1], (D,), jnp.float32), 0.099609375, 1.8984375).astype(jnp.bfloat16)
    query_weight = centred(keys[2], (D, QH * HD), D ** -0.5, 0.09375, ((1, 4),))
    keyval_weight = centred(keys[3], (D, 2 * KVH * HD), D ** -0.5, 0.09375, ((1, 4),))
    output_weight = noise_with(keys[4], (QH * HD, D), (QH * HD // 16) ** -0.5, 0.5, ((0, 4),), (0, 1, 4, 2.0))
    projection_down_weight = centred(part_keys[5], (ADAPTERS, D, RANK), D ** -0.5, 0.09375, ((0, 4), (1, 4)))
    query_up_weight = centred(part_keys[6], (ADAPTERS, RANK, QH * HD), RANK ** -0.5, 0.75, ((0, 4), (2, 4)))
    keyval_up_weight = centred(part_keys[7], (ADAPTERS, RANK, 2 * KVH * HD), RANK ** -0.5, 0.75, ((0, 4), (2, 4)))
    output_down_weight = centred(part_keys[8], (ADAPTERS, QH * HD, RANK), (QH * HD // 16) ** -0.5, 0.375, ((0, 4), (1, 4)))
    output_up_weight = centred(part_keys[9], (ADAPTERS, RANK, D), RANK ** -0.5, 0.75, ((0, 4), (2, 4)))
    adapter_ids = draw_adapter_ids(jax.random.fold_in(jax.random.fold_in(keys[14], part), 71), part)
    adapter_slot = draw_adapter_slot(jax.random.fold_in(jax.random.fold_in(keys[14], part), 71), part)
    kv_cache = draw_kv_cache(jax.random.fold_in(jax.random.fold_in(keys[14], part), 71), part)
    cache_len = uneven_parts(part_keys[13], REQS, REQS * CTX // 2, CTX, 2).astype(jnp.int32)
    return {"tokens": tokens, "norm_gain": norm_gain, "query_weight": query_weight, "keyval_weight": keyval_weight, "output_weight": output_weight, "projection_down_weight": projection_down_weight, "query_up_weight": query_up_weight, "keyval_up_weight": keyval_up_weight, "output_down_weight": output_down_weight, "output_up_weight": output_up_weight, "adapter_ids": adapter_ids, "adapter_slot": adapter_slot, "kv_cache": kv_cache, "cache_len": cache_len}


norm_eps = 1e-05
adapter_scale = 0.5
rope_theta = 500000.0

def rotate(vector, position):
    half_dim = vector.shape[-1] // 2
    frequency = rope_theta ** (-(2.0 * jnp.arange(half_dim, dtype=jnp.float32)) / vector.shape[-1])
    angles = position * frequency
    cosine = jnp.cos(angles)
    sine_part = jnp.sin(angles)
    first_half = vector[..., :half_dim]
    second = vector[..., half_dim:]
    return jnp.concatenate([first_half * cosine - second * sine_part, second * cosine + first_half * sine_part], axis=-1)

def attend_block(query_rows, keyval, cache_rows, lengths):
    req_count = cache_rows.shape[0]
    ctx_len = cache_rows.shape[1]
    per_group = QH // KVH
    score_scale = HD ** (-0.5)
    position = lengths.astype(jnp.float32)[:, None, None]
    rot_query = rotate(query_rows.reshape(req_count, QH, HD).astype(jnp.float32), position)
    rot_query = lax.optimization_barrier(rot_query.astype(jnp.bfloat16)).astype(jnp.float32)
    rot_query = rot_query.reshape(req_count, KVH, per_group, HD)
    rot_key = rotate(keyval[:, :KVH * HD].reshape(req_count, KVH, HD).astype(jnp.float32), position)
    rot_key = lax.optimization_barrier(rot_key.astype(jnp.bfloat16)).astype(jnp.float32)
    new_value = keyval[:, KVH * HD:].reshape(req_count, KVH, HD).astype(jnp.float32)
    old_keys = cache_rows[:, :, :KVH * HD].reshape(req_count, ctx_len, KVH, HD).astype(jnp.float32)
    old_values = cache_rows[:, :, KVH * HD:].reshape(req_count, ctx_len, KVH, HD).astype(jnp.float32)
    old_score = jnp.einsum('akgd,apkd->akgp', rot_query, old_keys) * score_scale
    new_score = jnp.einsum('akgd,akd->akg', rot_query, rot_key) * score_scale
    is_live = jnp.arange(ctx_len)[None, :] < lengths[:, None]
    old_score = jnp.where(is_live[:, None, None, :], old_score, -jnp.inf)
    peak_score = jnp.maximum(lax.optimization_barrier(jnp.max(old_score, axis=-1)), new_score)
    old_weight = jnp.exp(old_score - peak_score[..., None])
    new_weight = jnp.exp(new_score - peak_score)
    denominator = lax.optimization_barrier(jnp.sum(old_weight, axis=-1)) + new_weight
    old_prob = lax.optimization_barrier((old_weight / denominator[..., None]).astype(jnp.bfloat16)).astype(jnp.float32)
    new_prob = lax.optimization_barrier((new_weight / denominator).astype(jnp.bfloat16)).astype(jnp.float32)
    mixture = jnp.einsum('akgp,apkd->akgd', old_prob, old_values) + new_prob[..., None] * new_value[:, :, None, :]
    return mixture.reshape(req_count, QH * HD).astype(jnp.bfloat16)

def reference(tokens, norm_gain, query_weight, keyval_weight, output_weight, projection_down_weight, query_up_weight, keyval_up_weight, output_down_weight, output_up_weight, adapter_ids, adapter_slot, kv_cache, cache_len):
    widened = tokens.astype(jnp.float32)
    inv_rms = lax.rsqrt(lax.optimization_barrier(jnp.mean(widened * widened, axis=1, keepdims=True)) + norm_eps)
    normed = (widened * inv_rms * norm_gain.astype(jnp.float32)).astype(jnp.bfloat16)
    stored = adapter_slot[adapter_ids].astype(jnp.int32)

    def adapt_in(packed_pair):
        request_line, adapter_slot_index = packed_pair
        adapter_input = jnp.dot(request_line, projection_down_weight[adapter_slot_index], preferred_element_type=jnp.float32).astype(jnp.bfloat16)
        query_update = (adapter_scale * jnp.dot(adapter_input, query_up_weight[adapter_slot_index], preferred_element_type=jnp.float32)).astype(jnp.bfloat16)
        keyval_update = (adapter_scale * jnp.dot(adapter_input, keyval_up_weight[adapter_slot_index], preferred_element_type=jnp.float32)).astype(jnp.bfloat16)
        return (query_update, keyval_update)
    query_update, keyval_update = lax.map(adapt_in, (normed, stored))
    query_rows = (jnp.dot(normed, query_weight, preferred_element_type=jnp.float32) + lax.optimization_barrier(query_update).astype(jnp.float32)).astype(jnp.bfloat16)
    keyval = (jnp.dot(normed, keyval_weight, preferred_element_type=jnp.float32) + lax.optimization_barrier(keyval_update).astype(jnp.float32)).astype(jnp.bfloat16)
    block_rows = REQ_DEV // N_TP

    def attend_part(block_parts):
        return attend_block(block_parts[0], block_parts[1], block_parts[2], block_parts[3])
    attended = lax.map(attend_part, (query_rows.reshape(-1, block_rows, QH * HD), keyval.reshape(-1, block_rows, 2 * KVH * HD), kv_cache.reshape(-1, block_rows, CTX, 2 * KVH * HD), cache_len.reshape(-1, block_rows)))
    attended = attended.reshape(REQS, QH * HD)

    def adapt_out(packed_pair):
        request_line, adapter_slot_index = packed_pair
        adapter_output = jnp.dot(request_line, output_down_weight[adapter_slot_index], preferred_element_type=jnp.float32).astype(jnp.bfloat16)
        return (adapter_scale * jnp.dot(adapter_output, output_up_weight[adapter_slot_index], preferred_element_type=jnp.float32)).astype(jnp.bfloat16)
    delta_out = lax.map(adapt_out, (attended, stored))
    layer_out = (jnp.dot(attended, output_weight, preferred_element_type=jnp.float32) + lax.optimization_barrier(delta_out).astype(jnp.float32)).astype(jnp.bfloat16)
    return layer_out
```

```python
import functools

import jax
import jax.numpy as jnp
from jax import lax
from jax.experimental import pallas as pl
from jax.experimental.pallas import tpu as pltpu
from jax.sharding import PartitionSpec as P

QH = 32
KVH = 4
HD = 128
FETCH_OWN = 2


norm_eps = 1e-05
adapter_scale = 0.5
rope_theta = 500000.0


def rotate(vector, position):
    half_dim = vector.shape[-1] // 2
    frequency = rope_theta ** (-(2.0 * jnp.arange(half_dim, dtype=jnp.float32)) / vector.shape[-1])
    angles = position * frequency
    cosine = jnp.cos(angles)
    sine_part = jnp.sin(angles)
    first_half = vector[..., :half_dim]
    second = vector[..., half_dim:]
    return jnp.concatenate(
        [first_half * cosine - second * sine_part, second * cosine + first_half * sine_part],
        axis=-1,
    )


def attend_block(query_rows, keyval, cache_rows, lengths):
    req_count = cache_rows.shape[0]
    ctx_len = cache_rows.shape[1]
    per_group = QH // KVH
    score_scale = HD ** (-0.5)
    position = lengths.astype(jnp.float32)[:, None, None]
    rot_query = rotate(query_rows.reshape(req_count, QH, HD).astype(jnp.float32), position).astype(
        jnp.bfloat16
    )
    rot_query = rot_query.reshape(req_count, KVH, per_group, HD)
    rot_key = rotate(
        keyval[:, : KVH * HD].reshape(req_count, KVH, HD).astype(jnp.float32), position
    ).astype(jnp.bfloat16)
    new_value = keyval[:, KVH * HD :].reshape(req_count, KVH, HD)
    old_keys = cache_rows[:, :, : KVH * HD].reshape(req_count, ctx_len, KVH, HD)
    old_values = cache_rows[:, :, KVH * HD :].reshape(req_count, ctx_len, KVH, HD)
    old_score = (
        jnp.einsum("akgd,apkd->akgp", rot_query, old_keys, preferred_element_type=jnp.float32)
        * score_scale
    )
    new_score = (
        jnp.einsum("akgd,akd->akg", rot_query, rot_key, preferred_element_type=jnp.float32)
        * score_scale
    )
    is_live = jnp.arange(ctx_len)[None, :] < lengths[:, None]
    old_score = jnp.where(is_live[:, None, None, :], old_score, -jnp.inf)
    peak_score = jnp.maximum(jnp.max(old_score, axis=-1), new_score)
    old_weight = jnp.exp(old_score - peak_score[..., None])
    new_weight = jnp.exp(new_score - peak_score)
    denominator = jnp.sum(old_weight, axis=-1) + new_weight
    old_prob = (old_weight / denominator[..., None]).astype(jnp.bfloat16)
    new_prob = (new_weight / denominator).astype(jnp.bfloat16)
    mixture = jnp.einsum(
        "akgp,apkd->akgd", old_prob, old_values, preferred_element_type=jnp.float32
    )
    mixture = (
        mixture
        + new_prob.astype(jnp.float32)[..., None] * new_value.astype(jnp.float32)[:, :, None, :]
    )
    return mixture.reshape(req_count, QH * HD).astype(jnp.bfloat16)


def route_plan(adapter_ids, adapter_slot, owner_count, held_count):
    lookup = jnp.arange(adapter_slot.shape[0], dtype=jnp.int32)
    matches = adapter_ids[:, None] == lookup[None, :]
    slot_of = jnp.sum(jnp.where(matches, adapter_slot[None, :], 0), axis=1).reshape(owner_count, -1)
    holder = slot_of // held_count
    local_index = slot_of % held_count
    holder_hot = holder[:, :, None] == jnp.arange(owner_count, dtype=jnp.int32)[None, None, :]
    local_hot = local_index[:, :, None] == jnp.arange(held_count, dtype=jnp.int32)[None, None, :]
    both_hot = holder_hot[:, :, :, None] & local_hot[:, :, None, :]
    used_any = jnp.any(both_hot, axis=1)
    rank_in = jnp.cumsum(used_any.astype(jnp.int32), axis=2) - 1
    pick_ids = jnp.arange(FETCH_OWN, dtype=jnp.int32)
    chosen = used_any[..., None] & (rank_in[..., None] == pick_ids)
    wanted = jnp.sum(
        jnp.where(chosen, jnp.arange(held_count, dtype=jnp.int32)[None, None, :, None], 0), axis=2
    )
    row_pick = jnp.sum(jnp.where(both_hot, rank_in[:, None, :, :], 0), axis=(2, 3))
    row_place = (
        jnp.sum(jnp.where(holder_hot, jnp.cumsum(holder_hot.astype(jnp.int32), axis=1), 0), axis=2)
        - 1
    )
    return (holder, row_pick, row_place, wanted)


def rank_total_sum(partial_value):
    return lax.psum(partial_value, "tp")


def regroup(pieces):
    return lax.all_to_all(pieces, "tp", split_axis=0, concat_axis=0, tiled=True)


def per_device(
    tokens,
    norm_gain,
    query_weight,
    keyval_weight,
    output_weight,
    projection_down_weight,
    query_up_weight,
    keyval_up_weight,
    output_down_weight,
    output_up_weight,
    adapter_ids,
    adapter_slot,
    kv_cache,
    cache_len,
):
    owner_count = lax.axis_size("req")
    tp_count = lax.axis_size("tp")
    held_count = projection_down_weight.shape[0]
    my_owner = lax.axis_index("req")
    my_shard = lax.axis_index("tp")
    rows_here = tokens.shape[0]
    shard_width = tokens.shape[1]
    zeroed_half = jnp.zeros((), jnp.bfloat16)
    gathered, gain_whole = (
        lax.all_gather(tokens, "tp", axis=1, tiled=True),
        lax.all_gather(norm_gain, "tp", axis=0, tiled=True),
    )
    widened = gathered.astype(jnp.float32)
    inv_rms = lax.rsqrt(jnp.mean(widened * widened, axis=1, keepdims=True) + norm_eps)
    normed = (widened * inv_rms * gain_whole.astype(jnp.float32)).astype(jnp.bfloat16)
    normalized_share = lax.dynamic_slice_in_dim(normed, my_shard * shard_width, shard_width, 1)
    holder, row_pick, row_place, wanted = route_plan(
        adapter_ids, adapter_slot, owner_count, held_count
    )
    my_holder = lax.dynamic_index_in_dim(holder, my_owner, 0, keepdims=False)
    my_pick = lax.dynamic_index_in_dim(row_pick, my_owner, 0, keepdims=False)
    asked_for = lax.dynamic_index_in_dim(wanted, my_owner, 1, keepdims=False)

    def held_blocks(lookup_table):
        taken_rows = jnp.take(lookup_table, asked_for.reshape(-1), axis=0)
        return taken_rows.reshape(asked_for.shape + lookup_table.shape[1:])

    base_query = jnp.dot(normed, query_weight, preferred_element_type=jnp.float32)
    base_keyval = jnp.dot(normed, keyval_weight, preferred_element_type=jnp.float32)
    query_cols = query_weight.shape[1]
    got_down, got_query, got_keyval, got_odown, got_oup = (
        lax.all_to_all(
            held_blocks(projection_down_weight), "req", split_axis=0, concat_axis=0, tiled=True
        ),
        lax.all_to_all(
            held_blocks(query_up_weight), "req", split_axis=0, concat_axis=0, tiled=True
        ),
        lax.all_to_all(
            held_blocks(keyval_up_weight), "req", split_axis=0, concat_axis=0, tiled=True
        ),
        lax.all_to_all(
            held_blocks(output_down_weight), "req", split_axis=0, concat_axis=0, tiled=True
        ),
        lax.all_to_all(
            held_blocks(output_up_weight), "req", split_axis=0, concat_axis=0, tiled=True
        ),
    )
    fetched = owner_count * FETCH_OWN
    fetch_index = my_holder * FETCH_OWN + my_pick
    gather_hot_slots = fetch_index[:, None] == jnp.arange(fetched, dtype=jnp.int32)[None, :]
    down_matrix_table = got_down.reshape((fetched,) + got_down.shape[2:])
    adapter_share = jnp.einsum(
        "jg,vgi->jvi", normalized_share, down_matrix_table, preferred_element_type=jnp.float32
    )
    adapter_input = rank_total_sum(
        jnp.sum(jnp.where(gather_hot_slots[:, :, None], adapter_share, 0.0), axis=1)
    ).astype(jnp.bfloat16)
    scatter_input = jnp.where(
        gather_hot_slots.T[:, :, None], adapter_input[None, :, :], zeroed_half
    )
    query_update = (
        adapter_scale
        * jnp.einsum(
            "fre,feo->ro",
            scatter_input,
            got_query.reshape((fetched,) + got_query.shape[2:]),
            preferred_element_type=jnp.float32,
        )
    ).astype(jnp.bfloat16)
    keyval_update = (
        adapter_scale
        * jnp.einsum(
            "fre,feo->ro",
            scatter_input,
            got_keyval.reshape((fetched,) + got_keyval.shape[2:]),
            preferred_element_type=jnp.float32,
        )
    ).astype(jnp.bfloat16)
    query_rows = (base_query + lax.optimization_barrier(query_update).astype(jnp.float32)).astype(
        jnp.bfloat16
    )
    keyval = (base_keyval + lax.optimization_barrier(keyval_update).astype(jnp.float32)).astype(
        jnp.bfloat16
    )
    att_rows = kv_cache.shape[0]
    packed = jnp.concatenate([query_rows, keyval], axis=1).reshape(tp_count, att_rows, -1)
    arrived_heads = regroup(packed)
    head_query = jnp.transpose(arrived_heads[:, :, :query_cols], (1, 0, 2)).reshape(att_rows, -1)
    head_keyval = jnp.transpose(arrived_heads[:, :, query_cols:], (1, 0, 2)).reshape(att_rows, -1)
    attended_rows = attend_block(head_query, head_keyval, kv_cache, cache_len)
    back_heads = regroup(
        jnp.transpose(attended_rows.reshape(att_rows, tp_count, query_cols), (1, 0, 2))
    )
    attended = back_heads.reshape(rows_here, query_cols)
    odown_all = got_odown.reshape((fetched,) + got_odown.shape[2:])
    output_share = jnp.einsum(
        "rc,fce->rfe", attended, odown_all, preferred_element_type=jnp.float32
    )
    adapter_output = rank_total_sum(
        jnp.sum(jnp.where(gather_hot_slots[:, :, None], output_share, 0.0), axis=1)
    ).astype(jnp.bfloat16)
    scatter_output = jnp.where(
        gather_hot_slots.T[:, :, None], adapter_output[None, :, :], zeroed_half
    )
    delta_out = (
        adapter_scale
        * jnp.einsum(
            "fre,feo->ro",
            scatter_output,
            got_oup.reshape((fetched,) + got_oup.shape[2:]),
            preferred_element_type=jnp.float32,
        )
    ).astype(jnp.bfloat16)
    summed = lax.psum_scatter(
        jnp.einsum("rc,co->or", attended, output_weight, preferred_element_type=jnp.float32).astype(
            jnp.bfloat16
        ),
        "tp",
        scatter_dimension=0,
        tiled=True,
    ).astype(jnp.float32)
    return (summed.T + lax.optimization_barrier(delta_out).astype(jnp.float32)).astype(jnp.bfloat16)


MESH = pl.DeviceIdType.MESH
VMEM_BYTES = 60 * 1024 * 1024


def remote(src, dst, send_sem, recv_sem, **where_to):
    return pltpu.make_async_remote_copy(
        src_ref=src,
        dst_ref=dst,
        send_sem=send_sem,
        recv_sem=recv_sem,
        device_id=where_to,
        device_id_type=MESH,
    )


def dot_f32(left, right):
    return jnp.dot(left, right, preferred_element_type=jnp.float32)


def dot_t(left, right):
    return lax.dot_general(
        left, right, (((1,), (1,)), ((), ())), preferred_element_type=jnp.float32
    )


def greet(owner_count, tp_count):
    my_owner = lax.axis_index("req")
    my_shard = lax.axis_index("tp")
    barrier = pltpu.get_barrier_semaphore()
    for step in range(1, tp_count):
        pl.semaphore_signal(
            barrier,
            inc=1,
            device_id={"tp": lax.rem(my_shard + step, tp_count)},
            device_id_type=MESH,
        )
    for step in range(1, owner_count):
        pl.semaphore_signal(
            barrier,
            inc=1,
            device_id={"req": lax.rem(my_owner + step, owner_count)},
            device_id_type=MESH,
        )
    return barrier


def start_loads(pairs, load_sem):
    loads = []
    for number, (source, target) in enumerate(pairs):
        load = pltpu.make_async_copy(source, target, load_sem.at[number])
        load.start()
        loads.append(load)
    return loads


class AdapterRound:
    def __init__(self, owner_count, tp_count, ids, pick, gather, scatter, scratch):
        self.owner_count = owner_count
        self.tp_count = tp_count
        self.ids, self.pick, self.gather, self.scatter = ids, pick, gather, scatter
        (
            self.out_rows,
            self.in_rows,
            self.partial,
            self.out_delta,
            self.in_delta,
            self.row_sems,
            self.part_sems,
            self.delta_sems,
        ) = scratch
        self.my_owner = lax.axis_index("req")
        self.my_shard = lax.axis_index("tp")
        self.sent = []

    def ahead(self, step):
        return lax.rem(self.my_owner + step, self.owner_count)

    def behind(self, step):
        return lax.rem(self.my_owner - step + self.owner_count, self.owner_count)

    def send_rows(self, rows):
        self.row_copies = {}
        for step in range(1, self.owner_count):
            holder = self.ahead(step)
            self.out_rows[step] = dot_f32(self.gather[holder], rows).astype(jnp.bfloat16)
            copy = remote(
                self.out_rows.at[step],
                self.in_rows.at[step],
                self.row_sems.at[0, step],
                self.row_sems.at[1, step],
                req=holder,
            )
            copy.start()
            self.row_copies[step] = copy
            self.sent.append(copy)
        self.in_rows[0] = dot_f32(self.gather[self.my_owner], rows).astype(jnp.bfloat16)

    def sum_rank(self, down):
        rank = down.shape[1]
        self.part_copies = {}
        for pair in range(self.owner_count // 2):
            halves = []
            for step in (2 * pair, 2 * pair + 1):
                if step:
                    self.row_copies[step].wait_recv()
                asker = self.behind(step)
                both = jnp.concatenate(
                    [down[self.ids[2 * asker]], down[self.ids[2 * asker + 1]]], axis=0
                )
                share = dot_t(self.in_rows[step], both)
                halves.append(
                    jnp.where(self.pick[asker] > 0.0, share[:, rank:], share[:, :rank])
                )
            self.partial[0, pair] = jnp.concatenate(halves, axis=1)
            for step in range(1, self.tp_count):
                copy = remote(
                    self.partial.at[0, pair],
                    self.partial.at[step, pair],
                    self.part_sems.at[0, pair, step],
                    self.part_sems.at[1, pair, step],
                    tp=lax.rem(self.my_shard + step, self.tp_count),
                )
                copy.start()
                self.part_copies[pair, step] = copy
                self.sent.append(copy)

    def send_delta(self, ups):
        self.delta_copies = {}
        for pair in range(self.owner_count // 2):
            total = self.partial[0, pair]
            for step in range(1, self.tp_count):
                self.part_copies[pair, step].wait_recv()
                total = total + self.partial[step, pair]
            total = total.astype(jnp.bfloat16)
            rank = total.shape[1] // 2
            for half in range(2):
                step = 2 * pair + half
                asker = self.behind(step)
                first, second = self.ids[2 * asker], self.ids[2 * asker + 1]
                low_rank = total[:, half * rank : (half + 1) * rank]
                target = self.out_delta if step else self.in_delta
                start = 0
                for up in ups:
                    width = up.shape[2]
                    update = jnp.where(
                        self.pick[asker] > 0.0,
                        dot_f32(low_rank, up[second]),
                        dot_f32(low_rank, up[first]),
                    )
                    target[step, :, start : start + width] = (adapter_scale * update).astype(
                        jnp.bfloat16
                    )
                    start += width
                if step:
                    copy = remote(
                        self.out_delta.at[step],
                        self.in_delta.at[step],
                        self.delta_sems.at[0, step],
                        self.delta_sems.at[1, step],
                        req=asker,
                    )
                    copy.start()
                    self.delta_copies[step] = copy
                    self.sent.append(copy)

    def add_delta(self, base):
        delta = dot_f32(self.scatter[self.my_owner], self.in_delta[0])
        for step in range(1, self.owner_count):
            self.delta_copies[step].wait_recv()
            delta = delta + dot_f32(self.scatter[self.ahead(step)], self.in_delta[step])
        return base + delta

    def finish(self):
        for copy in self.sent:
            copy.wait_send()


def round_scratch(owner_count, tp_count, cap, width_in, rank, width_out):
    pairs = owner_count // 2
    return [
        pltpu.VMEM((owner_count, cap, width_in), jnp.bfloat16),
        pltpu.VMEM((owner_count, cap, width_in), jnp.bfloat16),
        pltpu.VMEM((tp_count, pairs, cap, 2 * rank), jnp.float32),
        pltpu.VMEM((owner_count, cap, width_out), jnp.bfloat16),
        pltpu.VMEM((owner_count, cap, width_out), jnp.bfloat16),
        pltpu.SemaphoreType.DMA((2, owner_count)),
        pltpu.SemaphoreType.DMA((2, pairs, tp_count)),
        pltpu.SemaphoreType.DMA((2, owner_count)),
    ]


ROUND_REFS = 8


def project_kernel(
    owner_count,
    tp_count,
    tokens,
    gain,
    ids,
    pick,
    gather,
    scatter,
    query_hbm,
    keyval_hbm,
    down_hbm,
    query_up_hbm,
    keyval_up_hbm,
    out,
    *scratch,
):
    round_refs, scratch = scratch[:ROUND_REFS], scratch[ROUND_REFS:]
    (
        query_weight,
        keyval_weight,
        down,
        query_up,
        keyval_up,
        load_sem,
        squares,
        square_sems,
        normed,
        normed_sems,
        heads_out,
        heads_in,
        heads_sems,
    ) = scratch
    my_shard = lax.axis_index("tp")
    rows, width = tokens.shape
    barrier = greet(owner_count, tp_count)
    loads = start_loads(
        (
            (down_hbm, down),
            (query_hbm, query_weight),
            (keyval_hbm, keyval_weight),
            (query_up_hbm, query_up),
            (keyval_up_hbm, keyval_up),
        ),
        load_sem,
    )
    adapters = AdapterRound(owner_count, tp_count, ids, pick, gather, scatter, round_refs)
    widened = tokens[...].astype(jnp.float32)
    own_square = jnp.sum(widened * widened, axis=1, keepdims=True)
    diagonal = lax.broadcasted_iota(jnp.int32, (rows, rows), 0) == lax.broadcasted_iota(
        jnp.int32, (rows, rows), 1
    )
    as_row = jnp.sum(jnp.where(diagonal, own_square, 0.0), axis=0, keepdims=True)
    squares[0] = jnp.broadcast_to(as_row, (8, rows))
    pl.semaphore_wait(barrier, owner_count + tp_count - 2)
    sent = []
    square_copies = {}
    for step in range(1, tp_count):
        copy = remote(
            squares.at[0],
            squares.at[step],
            square_sems.at[0, step],
            square_sems.at[1, step],
            tp=lax.rem(my_shard + step, tp_count),
        )
        copy.start()
        square_copies[step] = copy
        sent.append(copy)
    total_row = squares[0]
    for step in range(1, tp_count):
        square_copies[step].wait_recv()
        total_row = total_row + squares[step]
    total = jnp.sum(jnp.where(diagonal, total_row[:1], 0.0), axis=1, keepdims=True)
    inv_rms = lax.rsqrt(total / (width * tp_count) + norm_eps)
    own = (widened * inv_rms * gain[...].astype(jnp.float32)).astype(jnp.bfloat16)
    normed[0] = own
    adapters.send_rows(own)
    normed_copies = {}
    for step in range(1, tp_count):
        copy = remote(
            normed.at[0],
            normed.at[step],
            normed_sems.at[0, step],
            normed_sems.at[1, step],
            tp=lax.rem(my_shard + step, tp_count),
        )
        copy.start()
        normed_copies[step] = copy
        sent.append(copy)
    loads[0].wait()
    adapters.sum_rank(down)
    loads[3].wait()
    loads[4].wait()
    adapters.send_delta((query_up, keyval_up))
    loads[1].wait()
    loads[2].wait()
    base_query, base_keyval = 0.0, 0.0
    for step in range(tp_count):
        if step:
            normed_copies[step].wait_recv()
        source = lax.rem(my_shard - step + tp_count, tp_count)
        part = pl.ds(pl.multiple_of(source * width, width), width)
        share = normed[step]
        base_query = base_query + dot_f32(share, query_weight[part, :])
        base_keyval = base_keyval + dot_f32(share, keyval_weight[part, :])
    total = adapters.add_delta(jnp.concatenate([base_query, base_keyval], axis=1))
    att_rows = rows // tp_count
    heads_out[...] = total.astype(jnp.bfloat16).reshape(heads_out.shape)
    heads_copies = {}
    for step in range(1, tp_count):
        target = lax.rem(my_shard + step, tp_count)
        copy = remote(
            heads_out.at[target],
            heads_in.at[step],
            heads_sems.at[0, step],
            heads_sems.at[1, step],
            tp=target,
        )
        copy.start()
        heads_copies[step] = copy
        sent.append(copy)
    out[my_shard] = heads_out[my_shard]
    for step in range(1, tp_count):
        heads_copies[step].wait_recv()
        out[lax.rem(my_shard - step + tp_count, tp_count)] = heads_in[step]
    for copy in sent:
        copy.wait_send()
    adapters.finish()


def output_kernel(
    owner_count,
    tp_count,
    attended,
    ids,
    pick,
    gather,
    scatter,
    output_hbm,
    down_hbm,
    up_hbm,
    out,
    *scratch,
):
    round_refs, scratch = scratch[:ROUND_REFS], scratch[ROUND_REFS:]
    (
        output_weight,
        down,
        up,
        load_sem,
        heads_in,
        heads_sems,
        whole,
        share_out,
        share_in,
        share_sems,
    ) = scratch
    my_shard = lax.axis_index("tp")
    att_rows = attended.shape[0]
    width = whole.shape[1]
    barrier = greet(owner_count, tp_count)
    loads = start_loads(((down_hbm, down), (output_hbm, output_weight), (up_hbm, up)), load_sem)
    adapters = AdapterRound(owner_count, tp_count, ids, pick, gather, scatter, round_refs)
    pl.semaphore_wait(barrier, owner_count + tp_count - 2)
    sent = []
    heads_copies = {}
    for step in range(1, tp_count):
        target = lax.rem(my_shard + step, tp_count)
        copy = remote(
            attended.at[:, pl.ds(pl.multiple_of(target * width, width), width)],
            heads_in.at[step],
            heads_sems.at[0, step],
            heads_sems.at[1, step],
            tp=target,
        )
        copy.start()
        heads_copies[step] = copy
        sent.append(copy)
    whole[pl.ds(pl.multiple_of(my_shard * att_rows, att_rows), att_rows), :] = attended[
        :, pl.ds(pl.multiple_of(my_shard * width, width), width)
    ]
    for step in range(1, tp_count):
        heads_copies[step].wait_recv()
        source = lax.rem(my_shard - step + tp_count, tp_count)
        whole[pl.ds(pl.multiple_of(source * att_rows, att_rows), att_rows), :] = heads_in[step]
    rows = whole[...]
    adapters.send_rows(rows)
    loads[1].wait()
    out_width = out.shape[1]
    share_copies = {}
    for step in range(1, tp_count):
        target = lax.rem(my_shard + step, tp_count)
        part = pl.ds(pl.multiple_of(target * out_width, out_width), out_width)
        share_out[step] = dot_f32(rows, output_weight[:, part]).astype(jnp.bfloat16)
        copy = remote(
            share_out.at[step],
            share_in.at[step],
            share_sems.at[0, step],
            share_sems.at[1, step],
            tp=target,
        )
        copy.start()
        share_copies[step] = copy
        sent.append(copy)
    part = pl.ds(pl.multiple_of(my_shard * out_width, out_width), out_width)
    base = dot_f32(rows, output_weight[:, part])
    loads[0].wait()
    adapters.sum_rank(down)
    loads[2].wait()
    adapters.send_delta((up,))
    for step in range(1, tp_count):
        share_copies[step].wait_recv()
        base = base + share_in[step].astype(jnp.float32)
    out[...] = adapters.add_delta(base).astype(jnp.bfloat16)
    for copy in sent:
        copy.wait_send()
    adapters.finish()


def request_plan(adapter_ids, adapter_slot, owner_count, held_count, cap):
    my_owner = lax.axis_index("req")
    lookup = jnp.arange(adapter_slot.shape[0], dtype=jnp.int32)
    matches = adapter_ids[:, None] == lookup[None, :]
    slot_of = jnp.sum(jnp.where(matches, adapter_slot[None, :], 0), axis=1).reshape(owner_count, -1)
    holder = slot_of // held_count
    local = slot_of % held_count
    rows = holder.shape[1]
    earlier = jnp.arange(rows)[None, :] < jnp.arange(rows)[:, None]
    place_ids = jnp.arange(cap, dtype=jnp.int32)
    mine = lax.dynamic_index_in_dim(holder, my_owner, 0, keepdims=False)
    place = jnp.sum((earlier & (mine[None, :] == mine[:, None])).astype(jnp.int32), axis=1)
    goes = mine[None, :] == jnp.arange(owner_count, dtype=jnp.int32)[:, None]
    gather = goes[:, None, :] & (place[None, None, :] == place_ids[None, :, None])
    scatter = goes[:, :, None] & (place[None, :, None] == place_ids[None, None, :])
    comes = holder == my_owner
    low = jnp.min(jnp.where(comes, local, held_count - 1), axis=1)
    high = jnp.max(jnp.where(comes, local, 0), axis=1)
    ids = jnp.stack([low, high], axis=1).reshape(-1)
    taken = jnp.sum((earlier[None] & comes[:, None, :]).astype(jnp.int32), axis=2)
    second = comes & (local == high[:, None])
    pick = jnp.any(second[:, None, :] & (taken[:, None, :] == place_ids[None, :, None]), axis=2)
    return (
        ids,
        pick.astype(jnp.float32)[:, :, None],
        gather.astype(jnp.bfloat16),
        scatter.astype(jnp.bfloat16),
    )


VMEM_SPEC = pl.BlockSpec(memory_space=pltpu.VMEM)
SMEM_SPEC = pl.BlockSpec(memory_space=pltpu.SMEM)
HBM_SPEC = pl.BlockSpec(memory_space=pl.ANY)


def routed_device(
    tokens,
    norm_gain,
    query_weight,
    keyval_weight,
    output_weight,
    projection_down_weight,
    query_up_weight,
    keyval_up_weight,
    output_down_weight,
    output_up_weight,
    adapter_ids,
    adapter_slot,
    kv_cache,
    cache_len,
):
    owner_count = lax.axis_size("req")
    tp_count = lax.axis_size("tp")
    held_count, width, rank = projection_down_weight.shape
    rows = tokens.shape[0]
    cap = FETCH_OWN * rows // owner_count
    att_rows = kv_cache.shape[0]
    query_cols = query_weight.shape[1]
    head_cols = query_cols + keyval_weight.shape[1]
    out_cols = output_up_weight.shape[2]
    plan = request_plan(adapter_ids, adapter_slot, owner_count, held_count, cap)
    sems = pltpu.SemaphoreType.DMA
    arrived_heads = pl.pallas_call(
        functools.partial(project_kernel, owner_count, tp_count),
        out_shape=jax.ShapeDtypeStruct((tp_count, att_rows, head_cols), jnp.bfloat16),
        in_specs=[VMEM_SPEC] * 2 + [SMEM_SPEC] + [VMEM_SPEC] * 3 + [HBM_SPEC] * 5,
        out_specs=VMEM_SPEC,
        scratch_shapes=round_scratch(owner_count, tp_count, cap, width, rank, head_cols)
        + [
            pltpu.VMEM(query_weight.shape, jnp.bfloat16),
            pltpu.VMEM(keyval_weight.shape, jnp.bfloat16),
            pltpu.VMEM((held_count, rank, width), jnp.bfloat16),
            pltpu.VMEM(query_up_weight.shape, jnp.bfloat16),
            pltpu.VMEM(keyval_up_weight.shape, jnp.bfloat16),
            sems((5,)),
            pltpu.VMEM((tp_count, 8, rows), jnp.float32),
            sems((2, tp_count)),
            pltpu.VMEM((tp_count, rows, width), jnp.bfloat16),
            sems((2, tp_count)),
            pltpu.VMEM((tp_count, att_rows, head_cols), jnp.bfloat16),
            pltpu.VMEM((tp_count, att_rows, head_cols), jnp.bfloat16),
            sems((2, tp_count)),
        ],
        compiler_params=pltpu.CompilerParams(
            collective_id=1, has_side_effects=True, vmem_limit_bytes=VMEM_BYTES
        ),
    )(
        tokens,
        norm_gain[None, :],
        *plan,
        query_weight,
        keyval_weight,
        jnp.swapaxes(projection_down_weight, 1, 2),
        query_up_weight,
        keyval_up_weight,
    )
    attended_rows = attend(arrived_heads, kv_cache, cache_len, query_cols)
    return pl.pallas_call(
        functools.partial(output_kernel, owner_count, tp_count),
        out_shape=jax.ShapeDtypeStruct((rows, out_cols), jnp.bfloat16),
        in_specs=[VMEM_SPEC] + [SMEM_SPEC] + [VMEM_SPEC] * 3 + [HBM_SPEC] * 3,
        out_specs=VMEM_SPEC,
        scratch_shapes=round_scratch(owner_count, tp_count, cap, query_cols, rank, out_cols)
        + [
            pltpu.VMEM(output_weight.shape, jnp.bfloat16),
            pltpu.VMEM((held_count, rank, query_cols), jnp.bfloat16),
            pltpu.VMEM(output_up_weight.shape, jnp.bfloat16),
            sems((3,)),
            pltpu.VMEM((tp_count, att_rows, query_cols), jnp.bfloat16),
            sems((2, tp_count)),
            pltpu.VMEM((rows, query_cols), jnp.bfloat16),
            pltpu.VMEM((tp_count, rows, out_cols), jnp.bfloat16),
            pltpu.VMEM((tp_count, rows, out_cols), jnp.bfloat16),
            sems((2, tp_count)),
        ],
        compiler_params=pltpu.CompilerParams(
            collective_id=2, has_side_effects=True, vmem_limit_bytes=VMEM_BYTES
        ),
    )(
        attended_rows,
        *plan,
        output_weight,
        jnp.swapaxes(output_down_weight, 1, 2),
        output_up_weight,
    )


def attend(arrived_heads, kv_cache, cache_len, query_cols):
    att_rows = kv_cache.shape[0]
    head_query = jnp.transpose(arrived_heads[:, :, :query_cols], (1, 0, 2)).reshape(att_rows, -1)
    head_keyval = jnp.transpose(arrived_heads[:, :, query_cols:], (1, 0, 2)).reshape(att_rows, -1)
    return attend_block(head_query, head_keyval, kv_cache, cache_len)


def fits_kernels(mesh):
    tp_count, owner_count = mesh.shape["tp"], mesh.shape["req"]
    return (2 * KVH * HD // tp_count) % HD == 0 and tp_count <= KVH and owner_count % 2 == 0


def solution(mesh):
    in_specs = (
        P(("group", "req"), "tp"),
        P("tp"),
        P(None, "tp"),
        P(None, "tp"),
        P("tp", None),
        P(("group", "req"), "tp", None),
        P(("group", "req"), None, "tp"),
        P(("group", "req"), None, "tp"),
        P(("group", "req"), "tp", None),
        P(("group", "req"), None, "tp"),
        P("group"),
        P("group"),
        P(("group", "req", "tp"), None, None),
        P(("group", "req", "tp")),
    )
    out_specs = P(("group", "req"), "tp")
    return jax.shard_map(
        routed_device if fits_kernels(mesh) else per_device,
        mesh=mesh, in_specs=in_specs, out_specs=out_specs, check_vma=False
    )
```

```python
import functools
import math

import jax
import jax.numpy as jnp
from jax import lax
from jax.experimental import pallas as pl
from jax.experimental.pallas import tpu as pltpu
from jax.sharding import PartitionSpec as P

QH = 32
KVH = 4
HD = 128
FETCH_OWN = 2


norm_eps = 1e-05
adapter_scale = 0.5
rope_theta = 500000.0


def rotate(vector, position):
    half_dim = vector.shape[-1] // 2
    frequency = rope_theta ** (-(2.0 * jnp.arange(half_dim, dtype=jnp.float32)) / vector.shape[-1])
    angles = position * frequency
    cosine = jnp.cos(angles)
    sine_part = jnp.sin(angles)
    first_half = vector[..., :half_dim]
    second = vector[..., half_dim:]
    return jnp.concatenate(
        [first_half * cosine - second * sine_part, second * cosine + first_half * sine_part],
        axis=-1,
    )


def attend_block(query_rows, keyval, cache_rows, lengths):
    req_count = cache_rows.shape[0]
    ctx_len = cache_rows.shape[1]
    per_group = QH // KVH
    score_scale = HD ** (-0.5)
    position = lengths.astype(jnp.float32)[:, None, None]
    rot_query = rotate(query_rows.reshape(req_count, QH, HD).astype(jnp.float32), position).astype(
        jnp.bfloat16
    )
    rot_query = rot_query.reshape(req_count, KVH, per_group, HD)
    rot_key = rotate(
        keyval[:, : KVH * HD].reshape(req_count, KVH, HD).astype(jnp.float32), position
    ).astype(jnp.bfloat16)
    new_value = keyval[:, KVH * HD :].reshape(req_count, KVH, HD)
    old_keys = cache_rows[:, :, : KVH * HD].reshape(req_count, ctx_len, KVH, HD)
    old_values = cache_rows[:, :, KVH * HD :].reshape(req_count, ctx_len, KVH, HD)
    old_score = (
        jnp.einsum("akgd,apkd->akgp", rot_query, old_keys, preferred_element_type=jnp.float32)
        * score_scale
    )
    new_score = (
        jnp.einsum("akgd,akd->akg", rot_query, rot_key, preferred_element_type=jnp.float32)
        * score_scale
    )
    is_live = jnp.arange(ctx_len)[None, :] < lengths[:, None]
    old_score = jnp.where(is_live[:, None, None, :], old_score, -jnp.inf)
    peak_score = jnp.maximum(jnp.max(old_score, axis=-1), new_score)
    old_weight = jnp.exp(old_score - peak_score[..., None])
    new_weight = jnp.exp(new_score - peak_score)
    denominator = jnp.sum(old_weight, axis=-1) + new_weight
    old_prob = (old_weight / denominator[..., None]).astype(jnp.bfloat16)
    new_prob = (new_weight / denominator).astype(jnp.bfloat16)
    mixture = jnp.einsum(
        "akgp,apkd->akgd", old_prob, old_values, preferred_element_type=jnp.float32
    )
    mixture = (
        mixture
        + new_prob.astype(jnp.float32)[..., None] * new_value.astype(jnp.float32)[:, :, None, :]
    )
    return mixture.reshape(req_count, QH * HD).astype(jnp.bfloat16)


def route_plan(adapter_ids, adapter_slot, owner_count, held_count):
    lookup = jnp.arange(adapter_slot.shape[0], dtype=jnp.int32)
    matches = adapter_ids[:, None] == lookup[None, :]
    slot_of = jnp.sum(jnp.where(matches, adapter_slot[None, :], 0), axis=1).reshape(owner_count, -1)
    holder = slot_of // held_count
    local_index = slot_of % held_count
    holder_hot = holder[:, :, None] == jnp.arange(owner_count, dtype=jnp.int32)[None, None, :]
    local_hot = local_index[:, :, None] == jnp.arange(held_count, dtype=jnp.int32)[None, None, :]
    both_hot = holder_hot[:, :, :, None] & local_hot[:, :, None, :]
    used_any = jnp.any(both_hot, axis=1)
    rank_in = jnp.cumsum(used_any.astype(jnp.int32), axis=2) - 1
    pick_ids = jnp.arange(FETCH_OWN, dtype=jnp.int32)
    chosen = used_any[..., None] & (rank_in[..., None] == pick_ids)
    wanted = jnp.sum(
        jnp.where(chosen, jnp.arange(held_count, dtype=jnp.int32)[None, None, :, None], 0), axis=2
    )
    row_pick = jnp.sum(jnp.where(both_hot, rank_in[:, None, :, :], 0), axis=(2, 3))
    row_place = (
        jnp.sum(jnp.where(holder_hot, jnp.cumsum(holder_hot.astype(jnp.int32), axis=1), 0), axis=2)
        - 1
    )
    return (holder, row_pick, row_place, wanted)


def rank_total_sum(partial_value):
    return lax.psum(partial_value, "tp")


def regroup(pieces):
    return lax.all_to_all(pieces, "tp", split_axis=0, concat_axis=0, tiled=True)


def per_device(
    tokens,
    norm_gain,
    query_weight,
    keyval_weight,
    output_weight,
    projection_down_weight,
    query_up_weight,
    keyval_up_weight,
    output_down_weight,
    output_up_weight,
    adapter_ids,
    adapter_slot,
    kv_cache,
    cache_len,
):
    owner_count = lax.axis_size("req")
    tp_count = lax.axis_size("tp")
    held_count = projection_down_weight.shape[0]
    my_owner = lax.axis_index("req")
    my_shard = lax.axis_index("tp")
    rows_here = tokens.shape[0]
    shard_width = tokens.shape[1]
    zeroed_half = jnp.zeros((), jnp.bfloat16)
    gathered, gain_whole = (
        lax.all_gather(tokens, "tp", axis=1, tiled=True),
        lax.all_gather(norm_gain, "tp", axis=0, tiled=True),
    )
    widened = gathered.astype(jnp.float32)
    inv_rms = lax.rsqrt(jnp.mean(widened * widened, axis=1, keepdims=True) + norm_eps)
    normed = (widened * inv_rms * gain_whole.astype(jnp.float32)).astype(jnp.bfloat16)
    normalized_share = lax.dynamic_slice_in_dim(normed, my_shard * shard_width, shard_width, 1)
    holder, row_pick, row_place, wanted = route_plan(
        adapter_ids, adapter_slot, owner_count, held_count
    )
    my_holder = lax.dynamic_index_in_dim(holder, my_owner, 0, keepdims=False)
    my_pick = lax.dynamic_index_in_dim(row_pick, my_owner, 0, keepdims=False)
    asked_for = lax.dynamic_index_in_dim(wanted, my_owner, 1, keepdims=False)

    def held_blocks(lookup_table):
        taken_rows = jnp.take(lookup_table, asked_for.reshape(-1), axis=0)
        return taken_rows.reshape(asked_for.shape + lookup_table.shape[1:])

    base_query = jnp.dot(normed, query_weight, preferred_element_type=jnp.float32)
    base_keyval = jnp.dot(normed, keyval_weight, preferred_element_type=jnp.float32)
    query_cols = query_weight.shape[1]
    got_down, got_query, got_keyval, got_odown, got_oup = (
        lax.all_to_all(
            held_blocks(projection_down_weight), "req", split_axis=0, concat_axis=0, tiled=True
        ),
        lax.all_to_all(
            held_blocks(query_up_weight), "req", split_axis=0, concat_axis=0, tiled=True
        ),
        lax.all_to_all(
            held_blocks(keyval_up_weight), "req", split_axis=0, concat_axis=0, tiled=True
        ),
        lax.all_to_all(
            held_blocks(output_down_weight), "req", split_axis=0, concat_axis=0, tiled=True
        ),
        lax.all_to_all(
            held_blocks(output_up_weight), "req", split_axis=0, concat_axis=0, tiled=True
        ),
    )
    fetched = owner_count * FETCH_OWN
    fetch_index = my_holder * FETCH_OWN + my_pick
    gather_hot_slots = fetch_index[:, None] == jnp.arange(fetched, dtype=jnp.int32)[None, :]
    down_matrix_table = got_down.reshape((fetched,) + got_down.shape[2:])
    adapter_share = jnp.einsum(
        "jg,vgi->jvi", normalized_share, down_matrix_table, preferred_element_type=jnp.float32
    )
    adapter_input = rank_total_sum(
        jnp.sum(jnp.where(gather_hot_slots[:, :, None], adapter_share, 0.0), axis=1)
    ).astype(jnp.bfloat16)
    scatter_input = jnp.where(
        gather_hot_slots.T[:, :, None], adapter_input[None, :, :], zeroed_half
    )
    query_update = (
        adapter_scale
        * jnp.einsum(
            "fre,feo->ro",
            scatter_input,
            got_query.reshape((fetched,) + got_query.shape[2:]),
            preferred_element_type=jnp.float32,
        )
    ).astype(jnp.bfloat16)
    keyval_update = (
        adapter_scale
        * jnp.einsum(
            "fre,feo->ro",
            scatter_input,
            got_keyval.reshape((fetched,) + got_keyval.shape[2:]),
            preferred_element_type=jnp.float32,
        )
    ).astype(jnp.bfloat16)
    query_rows = (base_query + lax.optimization_barrier(query_update).astype(jnp.float32)).astype(
        jnp.bfloat16
    )
    keyval = (base_keyval + lax.optimization_barrier(keyval_update).astype(jnp.float32)).astype(
        jnp.bfloat16
    )
    att_rows = kv_cache.shape[0]
    packed = jnp.concatenate([query_rows, keyval], axis=1).reshape(tp_count, att_rows, -1)
    arrived_heads = regroup(packed)
    head_query = jnp.transpose(arrived_heads[:, :, :query_cols], (1, 0, 2)).reshape(att_rows, -1)
    head_keyval = jnp.transpose(arrived_heads[:, :, query_cols:], (1, 0, 2)).reshape(att_rows, -1)
    attended_rows = attend_block(head_query, head_keyval, kv_cache, cache_len)
    back_heads = regroup(
        jnp.transpose(attended_rows.reshape(att_rows, tp_count, query_cols), (1, 0, 2))
    )
    attended = back_heads.reshape(rows_here, query_cols)
    odown_all = got_odown.reshape((fetched,) + got_odown.shape[2:])
    output_share = jnp.einsum(
        "rc,fce->rfe", attended, odown_all, preferred_element_type=jnp.float32
    )
    adapter_output = rank_total_sum(
        jnp.sum(jnp.where(gather_hot_slots[:, :, None], output_share, 0.0), axis=1)
    ).astype(jnp.bfloat16)
    scatter_output = jnp.where(
        gather_hot_slots.T[:, :, None], adapter_output[None, :, :], zeroed_half
    )
    delta_out = (
        adapter_scale
        * jnp.einsum(
            "fre,feo->ro",
            scatter_output,
            got_oup.reshape((fetched,) + got_oup.shape[2:]),
            preferred_element_type=jnp.float32,
        )
    ).astype(jnp.bfloat16)
    summed = lax.psum_scatter(
        jnp.einsum("rc,co->or", attended, output_weight, preferred_element_type=jnp.float32).astype(
            jnp.bfloat16
        ),
        "tp",
        scatter_dimension=0,
        tiled=True,
    ).astype(jnp.float32)
    return (summed.T + lax.optimization_barrier(delta_out).astype(jnp.float32)).astype(jnp.bfloat16)


MESH = pl.DeviceIdType.MESH
VMEM_BYTES = 60 * 1024 * 1024


def remote(src, dst, send_sem, recv_sem, **where_to):
    return pltpu.make_async_remote_copy(
        src_ref=src,
        dst_ref=dst,
        send_sem=send_sem,
        recv_sem=recv_sem,
        device_id=where_to,
        device_id_type=MESH,
    )


def dot_f32(left, right):
    return jnp.dot(left, right, preferred_element_type=jnp.float32)


def dot_t(left, right):
    return lax.dot_general(
        left, right, (((1,), (1,)), ((), ())), preferred_element_type=jnp.float32
    )


def greet(owner_count, tp_count):
    my_owner = lax.axis_index("req")
    my_shard = lax.axis_index("tp")
    barrier = pltpu.get_barrier_semaphore()
    for step in range(1, tp_count):
        pl.semaphore_signal(
            barrier,
            inc=1,
            device_id={"tp": lax.rem(my_shard + step, tp_count)},
            device_id_type=MESH,
        )
    for step in range(1, owner_count):
        pl.semaphore_signal(
            barrier,
            inc=1,
            device_id={"req": lax.rem(my_owner + step, owner_count)},
            device_id_type=MESH,
        )
    return barrier


def start_loads(pairs, load_sem):
    loads = []
    for number, (source, target) in enumerate(pairs):
        load = pltpu.make_async_copy(source, target, load_sem.at[number])
        load.start()
        loads.append(load)
    return loads


class AdapterRound:
    def __init__(self, owner_count, tp_count, plan, scratch):
        self.owner_count = owner_count
        self.tp_count = tp_count
        self.named, self.pick, self.gather, self.scatter = plan
        (
            self.out_rows,
            self.in_rows,
            self.partial,
            self.out_delta,
            self.in_delta,
            self.row_sems,
            self.part_sems,
            self.delta_sems,
        ) = scratch
        self.my_owner = lax.axis_index("req")
        self.my_shard = lax.axis_index("tp")
        self.sent = []

    def ahead(self, step):
        return lax.rem(self.my_owner + step, self.owner_count)

    def behind(self, step):
        return lax.rem(self.my_owner - step + self.owner_count, self.owner_count)

    def send_rows(self, rows):
        self.row_copies = {}
        for step in range(1, self.owner_count):
            holder = self.ahead(step)
            self.out_rows[step] = dot_f32(self.gather[holder], rows).astype(jnp.bfloat16)
            copy = remote(
                self.out_rows.at[step],
                self.in_rows.at[step],
                self.row_sems.at[0, step],
                self.row_sems.at[1, step],
                req=holder,
            )
            copy.start()
            self.row_copies[step] = copy
            self.sent.append(copy)
        self.in_rows[0] = dot_f32(self.gather[self.my_owner], rows).astype(jnp.bfloat16)

    def sum_rank(self, down):
        rank = down.shape[1]
        self.part_copies = {}
        for pair in range(self.owner_count // 2):
            halves = []
            for step in (2 * pair, 2 * pair + 1):
                if step:
                    self.row_copies[step].wait_recv()
                first, second = self.named[step]
                both = jnp.concatenate([down[first], down[second]], axis=0)
                share = dot_t(self.in_rows[step], both)
                halves.append(jnp.where(self.pick[step] > 0, share[:, rank:], share[:, :rank]))
            self.partial[0, pair] = jnp.concatenate(halves, axis=1)
            for step in range(1, self.tp_count):
                copy = remote(
                    self.partial.at[0, pair],
                    self.partial.at[step, pair],
                    self.part_sems.at[0, pair, step],
                    self.part_sems.at[1, pair, step],
                    tp=lax.rem(self.my_shard + step, self.tp_count),
                )
                copy.start()
                self.part_copies[pair, step] = copy
                self.sent.append(copy)

    def send_delta(self, ups):
        self.delta_copies = {}
        for pair in range(self.owner_count // 2):
            total = self.partial[0, pair]
            for step in range(1, self.tp_count):
                self.part_copies[pair, step].wait_recv()
                total = total + self.partial[step, pair]
            total = total.astype(jnp.bfloat16)
            rank = total.shape[1] // 2
            for half in range(2):
                step = 2 * pair + half
                first, second = self.named[step]
                low_rank = total[:, half * rank : (half + 1) * rank]
                target = self.out_delta if step else self.in_delta
                start = 0
                for up in ups:
                    width = up.shape[2]
                    update = jnp.where(
                        self.pick[step] > 0,
                        dot_f32(low_rank, up[second]),
                        dot_f32(low_rank, up[first]),
                    )
                    target[step, :, start : start + width] = (adapter_scale * update).astype(
                        jnp.bfloat16
                    )
                    start += width
                if step:
                    copy = remote(
                        self.out_delta.at[step],
                        self.in_delta.at[step],
                        self.delta_sems.at[0, step],
                        self.delta_sems.at[1, step],
                        req=self.behind(step),
                    )
                    copy.start()
                    self.delta_copies[step] = copy
                    self.sent.append(copy)

    def add_delta(self, base):
        delta = dot_f32(self.scatter[self.my_owner], self.in_delta[0])
        for step in range(1, self.owner_count):
            self.delta_copies[step].wait_recv()
            delta = delta + dot_f32(self.scatter[self.ahead(step)], self.in_delta[step])
        return base + delta

    def finish(self):
        for copy in self.sent:
            copy.wait_send()


def round_scratch(owner_count, tp_count, cap, width_in, rank, width_out):
    pairs = owner_count // 2
    return [
        pltpu.VMEM((owner_count, cap, width_in), jnp.bfloat16),
        pltpu.VMEM((owner_count, cap, width_in), jnp.bfloat16),
        pltpu.VMEM((tp_count, pairs, cap, 2 * rank), jnp.float32),
        pltpu.VMEM((owner_count, cap, width_out), jnp.bfloat16),
        pltpu.VMEM((owner_count, cap, width_out), jnp.bfloat16),
        pltpu.SemaphoreType.DMA((2, owner_count)),
        pltpu.SemaphoreType.DMA((2, pairs, tp_count)),
        pltpu.SemaphoreType.DMA((2, owner_count)),
    ]


ROUND_REFS = 8


def make_plan(owner_count, held_count, cap, adapter_ids, adapter_slot, slots, pick, gather, scatter):
    my_owner = lax.axis_index("req")
    rows = adapter_ids.shape[1]
    lookups = adapter_slot.shape[1]

    def grid(shape):
        return [lax.broadcasted_iota(jnp.int32, shape, axis) for axis in (0, 1)]

    down, across = grid((rows, rows))
    down_of, across_of = grid((lookups, lookups))
    slot_down = jnp.sum(
        jnp.where(down_of == across_of, adapter_slot[...], 0), axis=1, keepdims=True
    )
    adapter_down, _ = grid((lookups, rows))
    for asker in range(owner_count):
        same = adapter_ids[asker : asker + 1, :] == adapter_down
        slots[asker : asker + 1, :] = jnp.sum(
            jnp.where(same, slot_down, 0), axis=0, keepdims=True
        )

    def turned(row):
        return jnp.sum(jnp.where(down == across, row, 0), axis=1, keepdims=True)

    def inside(values, holder):
        return (values >= holder * held_count) & (values < (holder + 1) * held_count)

    place_down, _ = grid((cap, rows))
    _, place_across = grid((rows, cap))
    mine = slots[pl.ds(my_owner, 1), :]
    mine_down = turned(mine)
    for holder in range(owner_count):
        goes, goes_down = inside(mine, holder), inside(mine_down, holder)
        place = jnp.sum(
            jnp.where((down < across) & goes_down, 1, 0), axis=0, keepdims=True
        )
        place_of_down = jnp.sum(
            jnp.where((across < down) & goes, 1, 0), axis=1, keepdims=True
        )
        gather[holder] = jnp.where(goes & (place == place_down), 1.0, 0.0).astype(jnp.bfloat16)
        scatter[holder] = jnp.where(
            goes_down & (place_of_down == place_across), 1.0, 0.0
        ).astype(jnp.bfloat16)
    named = []
    for step in range(owner_count):
        asker = lax.rem(my_owner - step + owner_count, owner_count)
        asked = slots[pl.ds(asker, 1), :]
        asked_down = turned(asked)
        comes, comes_down = inside(asked, my_owner), inside(asked_down, my_owner)
        local = asked - my_owner * held_count
        low = jnp.min(jnp.where(comes, local, held_count - 1))
        high = jnp.max(jnp.where(comes, local, 0))
        place = jnp.sum(
            jnp.where((down < across) & comes_down, 1, 0), axis=0, keepdims=True
        )
        second = comes & (local == high) & (place == place_down)
        pick[step] = jnp.sum(jnp.where(second, 1, 0), axis=1, keepdims=True)
        named.append((low, high))
    return named


def attend_rows(cache, lengths, queries, keys, values, mixed):
    count, ctx_len, cache_width = cache.shape
    half = cache_width // 2
    per_group = QH // KVH
    score_scale = HD ** (-0.5)
    together = math.gcd(count, 4)
    own_block = lax.broadcasted_iota(jnp.int32, (QH, half), 0) // per_group == (
        lax.broadcasted_iota(jnp.int32, (QH, half), 1) // HD
    )
    head_group = lax.broadcasted_iota(jnp.int32, (QH, HD), 0) // per_group
    position = lax.broadcasted_iota(jnp.int32, (QH, ctx_len), 1)

    def body(block, carry):
        scores, news = [], []
        for inner in range(together):
            request = block * together + inner
            query = queries[request].astype(jnp.bfloat16)
            spread = jnp.where(own_block, jnp.concatenate([query] * KVH, axis=1), 0)
            score = dot_t(spread.astype(jnp.bfloat16), cache[request, :, :half]) * score_scale
            scores.append(jnp.where(position < lengths[request], score, -jnp.inf))
            news.append(
                jnp.sum(
                    query.astype(jnp.float32)
                    * keys[request].astype(jnp.bfloat16).astype(jnp.float32),
                    axis=1,
                    keepdims=True,
                )
                * score_scale
            )
        score = jnp.concatenate(scores, axis=0)
        new = jnp.concatenate(news, axis=0)
        peak = jnp.maximum(jnp.max(score, axis=1, keepdims=True), new)
        weight = jnp.exp(score - peak)
        new_weight = jnp.exp(new - peak)
        total = jnp.sum(weight, axis=1, keepdims=True) + new_weight
        prob = (weight / total).astype(jnp.bfloat16)
        new_prob = (new_weight / total).astype(jnp.bfloat16).astype(jnp.float32)
        for inner in range(together):
            request = block * together + inner
            part = slice(inner * QH, (inner + 1) * QH)
            wide = dot_f32(prob[part], cache[request, :, half:])
            result = new_prob[part] * values[request]
            for group in range(KVH):
                result = result + jnp.where(
                    head_group == group, wide[:, group * HD : (group + 1) * HD], 0.0
                )
            mixed[request] = result
        return carry

    lax.fori_loop(0, count // together, body, 0)


def layer_kernel(
    owner_count,
    tp_count,
    tokens,
    gain,
    adapter_ids,
    adapter_slot,
    turns,
    lengths,
    query_hbm,
    keyval_hbm,
    output_hbm,
    down_hbm,
    query_up_hbm,
    keyval_up_hbm,
    output_down_hbm,
    output_up_hbm,
    cache_hbm,
    out,
    *scratch,
):
    first_refs, scratch = scratch[:ROUND_REFS], scratch[ROUND_REFS:]
    second_refs, scratch = scratch[:ROUND_REFS], scratch[ROUND_REFS:]
    (
        query_weight,
        keyval_weight,
        output_weight,
        down,
        wide_up,
        keyval_up,
        cache,
        load_sem,
        slots,
        pick,
        gather,
        scatter,
        squares,
        square_sems,
        normed,
        normed_sems,
        heads_out,
        heads_in,
        heads_sems,
        queries,
        keys,
        values,
        mixed,
        mixed_out,
        mixed_in,
        mixed_sems,
        attended,
        share_out,
        share_in,
        share_sems,
    ) = scratch
    my_shard = lax.axis_index("tp")
    rows, width = tokens.shape
    held_count = down.shape[0]
    cap = gather.shape[1]
    barrier = greet(owner_count, tp_count)
    loads = start_loads(
        (
            (down_hbm, down),
            (query_hbm, query_weight),
            (keyval_hbm, keyval_weight),
            (query_up_hbm, wide_up),
            (keyval_up_hbm, keyval_up),
            (cache_hbm, cache),
            (output_hbm, output_weight),
        ),
        load_sem,
    )
    late_loads = (
        pltpu.make_async_copy(output_down_hbm, down, load_sem.at[len(loads)]),
        pltpu.make_async_copy(output_up_hbm, wide_up, load_sem.at[len(loads) + 1]),
    )
    sent = []

    def swap(source_of, target, sems):
        copies = {}
        for step in range(1, tp_count):
            peer = lax.rem(my_shard + step, tp_count)
            copies[step] = remote(
                source_of(step, peer), target.at[step], sems.at[0, step], sems.at[1, step], tp=peer
            )
            copies[step].start()
            sent.append(copies[step])
        return copies

    def sender(step):
        return lax.rem(my_shard - step + tp_count, tp_count)

    widened = tokens[...].astype(jnp.float32)
    own_square = jnp.sum(widened * widened, axis=1, keepdims=True)
    diagonal = lax.broadcasted_iota(jnp.int32, (rows, rows), 0) == lax.broadcasted_iota(
        jnp.int32, (rows, rows), 1
    )
    as_row = jnp.sum(jnp.where(diagonal, own_square, 0.0), axis=0, keepdims=True)
    squares[0] = jnp.broadcast_to(as_row, (8, rows))
    pl.semaphore_wait(barrier, owner_count + tp_count - 2)
    square_copies = swap(lambda step, peer: squares.at[0], squares, square_sems)
    named = make_plan(
        owner_count, held_count, cap, adapter_ids, adapter_slot, slots, pick, gather, scatter
    )
    plan = (named, pick, gather, scatter)
    first = AdapterRound(owner_count, tp_count, plan, first_refs)
    second = AdapterRound(owner_count, tp_count, plan, second_refs)
    total_row = squares[0]
    for step in range(1, tp_count):
        square_copies[step].wait_recv()
        total_row = total_row + squares[step]
    total = jnp.sum(jnp.where(diagonal, total_row[:1], 0.0), axis=1, keepdims=True)
    inv_rms = lax.rsqrt(total / (width * tp_count) + norm_eps)
    own = (widened * inv_rms * gain[...].astype(jnp.float32)).astype(jnp.bfloat16)
    normed[0] = own
    first.send_rows(own)
    normed_copies = swap(lambda step, peer: normed.at[0], normed, normed_sems)
    loads[0].wait()
    first.sum_rank(down)
    late_loads[0].start()
    loads[3].wait()
    loads[4].wait()
    first.send_delta((wide_up, keyval_up))
    late_loads[1].start()
    loads[1].wait()
    loads[2].wait()
    base_query, base_keyval = 0.0, 0.0
    for step in range(tp_count):
        if step:
            normed_copies[step].wait_recv()
        part = pl.ds(pl.multiple_of(sender(step) * width, width), width)
        share = normed[step]
        base_query = base_query + dot_f32(share, query_weight[part, :])
        base_keyval = base_keyval + dot_f32(share, keyval_weight[part, :])
    total = first.add_delta(jnp.concatenate([base_query, base_keyval], axis=1))
    heads_out[...] = total.astype(jnp.bfloat16).reshape(heads_out.shape)
    heads_copies = swap(lambda step, peer: heads_out.at[peer], heads_in, heads_sems)
    heads_in[0] = heads_out[my_shard]
    cosine, sine = turns[:, :HD], turns[:, HD:]

    def rotated(vector):
        half = HD // 2
        swapped = jnp.concatenate([vector[:, half:], vector[:, :half]], axis=1)
        return vector * cosine + swapped * sine

    query_cols = query_weight.shape[1]
    per_group = QH // KVH
    per_shard = query_cols // HD
    keyval_shard = keyval_weight.shape[1] // HD
    for step in range(1, tp_count):
        heads_copies[step].wait_recv()
    for shard in range(tp_count):
        slot = lax.rem(my_shard - shard + tp_count, tp_count)
        block = heads_in[slot].astype(jnp.float32)
        for head in range(per_shard):
            queries[:, shard * per_shard + head, :] = rotated(
                block[:, head * HD : (head + 1) * HD]
            )
        for head in range(keyval_shard):
            number = shard * keyval_shard + head
            start = query_cols + head * HD
            vector = block[:, start : start + HD]
            target, vector = (keys, rotated(vector)) if number < KVH else (values, vector)
            for copy_of in range(per_group):
                target[:, (number % KVH) * per_group + copy_of, :] = vector
    loads[5].wait()
    attend_rows(cache, lengths, queries, keys, values, mixed)
    for shard in range(tp_count):
        for head in range(per_shard):
            mixed_out[shard, :, head * HD : (head + 1) * HD] = mixed[
                :, shard * per_shard + head, :
            ].astype(jnp.bfloat16)
    mixed_copies = swap(lambda step, peer: mixed_out.at[peer], mixed_in, mixed_sems)
    mixed_in[0] = mixed_out[my_shard]
    att_rows = mixed_in.shape[1]
    for step in range(tp_count):
        if step:
            mixed_copies[step].wait_recv()
        attended[pl.ds(pl.multiple_of(sender(step) * att_rows, att_rows), att_rows), :] = mixed_in[
            step
        ]
    own = attended[...]
    second.send_rows(own)
    loads[6].wait()
    out_width = out.shape[1]

    def output_share(peer):
        return dot_f32(
            own, output_weight[:, pl.ds(pl.multiple_of(peer * out_width, out_width), out_width)]
        )

    def staged_share(step, peer):
        share_out[step] = output_share(peer).astype(jnp.bfloat16)
        return share_out.at[step]

    share_copies = swap(staged_share, share_in, share_sems)
    base = output_share(my_shard)
    late_loads[0].wait()
    second.sum_rank(down)
    late_loads[1].wait()
    second.send_delta((wide_up,))
    for step in range(1, tp_count):
        share_copies[step].wait_recv()
        base = base + share_in[step].astype(jnp.float32)
    out[...] = second.add_delta(base).astype(jnp.bfloat16)
    for copy in sent:
        copy.wait_send()
    first.finish()
    second.finish()


def turn_table(lengths):
    half_dim = HD // 2
    frequency = rope_theta ** (-(2.0 * jnp.arange(half_dim, dtype=jnp.float32)) / HD)
    angles = lengths.astype(jnp.float32)[:, None] * frequency
    cosine, sine = jnp.cos(angles), jnp.sin(angles)
    return jnp.concatenate([cosine, cosine, -sine, sine], axis=1)


VMEM_SPEC = pl.BlockSpec(memory_space=pltpu.VMEM)
SMEM_SPEC = pl.BlockSpec(memory_space=pltpu.SMEM)
HBM_SPEC = pl.BlockSpec(memory_space=pl.ANY)


def routed_device(
    tokens,
    norm_gain,
    query_weight,
    keyval_weight,
    output_weight,
    projection_down_weight,
    query_up_weight,
    keyval_up_weight,
    output_down_weight,
    output_up_weight,
    adapter_ids,
    adapter_slot,
    kv_cache,
    cache_len,
):
    owner_count = lax.axis_size("req")
    tp_count = lax.axis_size("tp")
    held_count, width, rank = projection_down_weight.shape
    rows = tokens.shape[0]
    cap = FETCH_OWN * rows // owner_count
    att_rows = kv_cache.shape[0]
    query_cols = query_weight.shape[1]
    head_cols = query_cols + keyval_weight.shape[1]
    out_cols = output_up_weight.shape[2]
    sems = pltpu.SemaphoreType.DMA
    vmem = pltpu.VMEM
    return pl.pallas_call(
        functools.partial(layer_kernel, owner_count, tp_count),
        out_shape=jax.ShapeDtypeStruct((rows, out_cols), jnp.bfloat16),
        in_specs=[VMEM_SPEC] * 5 + [SMEM_SPEC] + [HBM_SPEC] * 9,
        out_specs=VMEM_SPEC,
        scratch_shapes=round_scratch(owner_count, tp_count, cap, width, rank, head_cols)
        + round_scratch(owner_count, tp_count, cap, query_cols, rank, out_cols)
        + [
            vmem(query_weight.shape, jnp.bfloat16),
            vmem(keyval_weight.shape, jnp.bfloat16),
            vmem(output_weight.shape, jnp.bfloat16),
            vmem((held_count, rank, width), jnp.bfloat16),
            vmem(query_up_weight.shape, jnp.bfloat16),
            vmem(keyval_up_weight.shape, jnp.bfloat16),
            vmem(kv_cache.shape, jnp.bfloat16),
            sems((9,)),
            vmem((owner_count, rows), jnp.int32),
            vmem((owner_count, cap, 1), jnp.int32),
            vmem((owner_count, cap, rows), jnp.bfloat16),
            vmem((owner_count, rows, cap), jnp.bfloat16),
            vmem((tp_count, 8, rows), jnp.float32),
            sems((2, tp_count)),
            vmem((tp_count, rows, width), jnp.bfloat16),
            sems((2, tp_count)),
            vmem((tp_count, att_rows, head_cols), jnp.bfloat16),
            vmem((tp_count, att_rows, head_cols), jnp.bfloat16),
            sems((2, tp_count)),
            vmem((att_rows, QH, HD), jnp.float32),
            vmem((att_rows, QH, HD), jnp.float32),
            vmem((att_rows, QH, HD), jnp.float32),
            vmem((att_rows, QH, HD), jnp.float32),
            vmem((tp_count, att_rows, query_cols), jnp.bfloat16),
            vmem((tp_count, att_rows, query_cols), jnp.bfloat16),
            sems((2, tp_count)),
            vmem((rows, query_cols), jnp.bfloat16),
            vmem((tp_count, rows, out_cols), jnp.bfloat16),
            vmem((tp_count, rows, out_cols), jnp.bfloat16),
            sems((2, tp_count)),
        ],
        compiler_params=pltpu.CompilerParams(
            collective_id=1, has_side_effects=True, vmem_limit_bytes=VMEM_BYTES
        ),
    )(
        tokens,
        norm_gain[None, :],
        adapter_ids.reshape(owner_count, rows),
        adapter_slot[None, :],
        turn_table(cache_len),
        cache_len,
        query_weight,
        keyval_weight,
        output_weight,
        jnp.swapaxes(projection_down_weight, 1, 2),
        query_up_weight,
        keyval_up_weight,
        jnp.swapaxes(output_down_weight, 1, 2),
        output_up_weight,
        kv_cache,
    )


def fits_kernels(mesh):
    tp_count, owner_count = mesh.shape["tp"], mesh.shape["req"]
    return (2 * KVH * HD // tp_count) % HD == 0 and tp_count <= KVH and owner_count % 2 == 0


def solution(mesh):
    in_specs = (
        P(("group", "req"), "tp"),
        P("tp"),
        P(None, "tp"),
        P(None, "tp"),
        P("tp", None),
        P(("group", "req"), "tp", None),
        P(("group", "req"), None, "tp"),
        P(("group", "req"), None, "tp"),
        P(("group", "req"), "tp", None),
        P(("group", "req"), None, "tp"),
        P("group"),
        P("group"),
        P(("group", "req", "tp"), None, None),
        P(("group", "req", "tp")),
    )
    out_specs = P(("group", "req"), "tp")
    return jax.shard_map(
        routed_device if fits_kernels(mesh) else per_device,
        mesh=mesh, in_specs=in_specs, out_specs=out_specs, check_vma=False
    )
```

```python
import functools
import math

import jax
import jax.numpy as jnp
from jax import lax
from jax.experimental import pallas as pl
from jax.experimental.pallas import tpu as pltpu
from jax.sharding import PartitionSpec as P

QH = 32
KVH = 4
HD = 128
FETCH_OWN = 2


norm_eps = 1e-05
adapter_scale = 0.5
rope_theta = 500000.0


def rotate(vector, position):
    half_dim = vector.shape[-1] // 2
    frequency = rope_theta ** (-(2.0 * jnp.arange(half_dim, dtype=jnp.float32)) / vector.shape[-1])
    angles = position * frequency
    cosine = jnp.cos(angles)
    sine_part = jnp.sin(angles)
    first_half = vector[..., :half_dim]
    second = vector[..., half_dim:]
    return jnp.concatenate(
        [first_half * cosine - second * sine_part, second * cosine + first_half * sine_part],
        axis=-1,
    )


def attend_block(query_rows, keyval, cache_rows, lengths):
    req_count = cache_rows.shape[0]
    ctx_len = cache_rows.shape[1]
    per_group = QH // KVH
    score_scale = HD ** (-0.5)
    position = lengths.astype(jnp.float32)[:, None, None]
    rot_query = rotate(query_rows.reshape(req_count, QH, HD).astype(jnp.float32), position).astype(
        jnp.bfloat16
    )
    rot_query = rot_query.reshape(req_count, KVH, per_group, HD)
    rot_key = rotate(
        keyval[:, : KVH * HD].reshape(req_count, KVH, HD).astype(jnp.float32), position
    ).astype(jnp.bfloat16)
    new_value = keyval[:, KVH * HD :].reshape(req_count, KVH, HD)
    old_keys = cache_rows[:, :, : KVH * HD].reshape(req_count, ctx_len, KVH, HD)
    old_values = cache_rows[:, :, KVH * HD :].reshape(req_count, ctx_len, KVH, HD)
    old_score = (
        jnp.einsum("akgd,apkd->akgp", rot_query, old_keys, preferred_element_type=jnp.float32)
        * score_scale
    )
    new_score = (
        jnp.einsum("akgd,akd->akg", rot_query, rot_key, preferred_element_type=jnp.float32)
        * score_scale
    )
    is_live = jnp.arange(ctx_len)[None, :] < lengths[:, None]
    old_score = jnp.where(is_live[:, None, None, :], old_score, -jnp.inf)
    peak_score = jnp.maximum(jnp.max(old_score, axis=-1), new_score)
    old_weight = jnp.exp(old_score - peak_score[..., None])
    new_weight = jnp.exp(new_score - peak_score)
    denominator = jnp.sum(old_weight, axis=-1) + new_weight
    old_prob = (old_weight / denominator[..., None]).astype(jnp.bfloat16)
    new_prob = (new_weight / denominator).astype(jnp.bfloat16)
    mixture = jnp.einsum(
        "akgp,apkd->akgd", old_prob, old_values, preferred_element_type=jnp.float32
    )
    mixture = (
        mixture
        + new_prob.astype(jnp.float32)[..., None] * new_value.astype(jnp.float32)[:, :, None, :]
    )
    return mixture.reshape(req_count, QH * HD).astype(jnp.bfloat16)


def route_plan(adapter_ids, adapter_slot, owner_count, held_count):
    lookup = jnp.arange(adapter_slot.shape[0], dtype=jnp.int32)
    matches = adapter_ids[:, None] == lookup[None, :]
    slot_of = jnp.sum(jnp.where(matches, adapter_slot[None, :], 0), axis=1).reshape(owner_count, -1)
    holder = slot_of // held_count
    local_index = slot_of % held_count
    holder_hot = holder[:, :, None] == jnp.arange(owner_count, dtype=jnp.int32)[None, None, :]
    local_hot = local_index[:, :, None] == jnp.arange(held_count, dtype=jnp.int32)[None, None, :]
    both_hot = holder_hot[:, :, :, None] & local_hot[:, :, None, :]
    used_any = jnp.any(both_hot, axis=1)
    rank_in = jnp.cumsum(used_any.astype(jnp.int32), axis=2) - 1
    pick_ids = jnp.arange(FETCH_OWN, dtype=jnp.int32)
    chosen = used_any[..., None] & (rank_in[..., None] == pick_ids)
    wanted = jnp.sum(
        jnp.where(chosen, jnp.arange(held_count, dtype=jnp.int32)[None, None, :, None], 0), axis=2
    )
    row_pick = jnp.sum(jnp.where(both_hot, rank_in[:, None, :, :], 0), axis=(2, 3))
    row_place = (
        jnp.sum(jnp.where(holder_hot, jnp.cumsum(holder_hot.astype(jnp.int32), axis=1), 0), axis=2)
        - 1
    )
    return (holder, row_pick, row_place, wanted)


def rank_total_sum(partial_value):
    return lax.psum(partial_value, "tp")


def regroup(pieces):
    return lax.all_to_all(pieces, "tp", split_axis=0, concat_axis=0, tiled=True)


def per_device(
    tokens,
    norm_gain,
    query_weight,
    keyval_weight,
    output_weight,
    projection_down_weight,
    query_up_weight,
    keyval_up_weight,
    output_down_weight,
    output_up_weight,
    adapter_ids,
    adapter_slot,
    kv_cache,
    cache_len,
):
    owner_count = lax.axis_size("req")
    tp_count = lax.axis_size("tp")
    held_count = projection_down_weight.shape[0]
    my_owner = lax.axis_index("req")
    my_shard = lax.axis_index("tp")
    rows_here = tokens.shape[0]
    shard_width = tokens.shape[1]
    zeroed_half = jnp.zeros((), jnp.bfloat16)
    gathered, gain_whole = (
        lax.all_gather(tokens, "tp", axis=1, tiled=True),
        lax.all_gather(norm_gain, "tp", axis=0, tiled=True),
    )
    widened = gathered.astype(jnp.float32)
    inv_rms = lax.rsqrt(jnp.mean(widened * widened, axis=1, keepdims=True) + norm_eps)
    normed = (widened * inv_rms * gain_whole.astype(jnp.float32)).astype(jnp.bfloat16)
    normalized_share = lax.dynamic_slice_in_dim(normed, my_shard * shard_width, shard_width, 1)
    holder, row_pick, row_place, wanted = route_plan(
        adapter_ids, adapter_slot, owner_count, held_count
    )
    my_holder = lax.dynamic_index_in_dim(holder, my_owner, 0, keepdims=False)
    my_pick = lax.dynamic_index_in_dim(row_pick, my_owner, 0, keepdims=False)
    asked_for = lax.dynamic_index_in_dim(wanted, my_owner, 1, keepdims=False)

    def held_blocks(lookup_table):
        taken_rows = jnp.take(lookup_table, asked_for.reshape(-1), axis=0)
        return taken_rows.reshape(asked_for.shape + lookup_table.shape[1:])

    base_query = jnp.dot(normed, query_weight, preferred_element_type=jnp.float32)
    base_keyval = jnp.dot(normed, keyval_weight, preferred_element_type=jnp.float32)
    query_cols = query_weight.shape[1]
    got_down, got_query, got_keyval, got_odown, got_oup = (
        lax.all_to_all(
            held_blocks(projection_down_weight), "req", split_axis=0, concat_axis=0, tiled=True
        ),
        lax.all_to_all(
            held_blocks(query_up_weight), "req", split_axis=0, concat_axis=0, tiled=True
        ),
        lax.all_to_all(
            held_blocks(keyval_up_weight), "req", split_axis=0, concat_axis=0, tiled=True
        ),
        lax.all_to_all(
            held_blocks(output_down_weight), "req", split_axis=0, concat_axis=0, tiled=True
        ),
        lax.all_to_all(
            held_blocks(output_up_weight), "req", split_axis=0, concat_axis=0, tiled=True
        ),
    )
    fetched = owner_count * FETCH_OWN
    fetch_index = my_holder * FETCH_OWN + my_pick
    gather_hot_slots = fetch_index[:, None] == jnp.arange(fetched, dtype=jnp.int32)[None, :]
    down_matrix_table = got_down.reshape((fetched,) + got_down.shape[2:])
    adapter_share = jnp.einsum(
        "jg,vgi->jvi", normalized_share, down_matrix_table, preferred_element_type=jnp.float32
    )
    adapter_input = rank_total_sum(
        jnp.sum(jnp.where(gather_hot_slots[:, :, None], adapter_share, 0.0), axis=1)
    ).astype(jnp.bfloat16)
    scatter_input = jnp.where(
        gather_hot_slots.T[:, :, None], adapter_input[None, :, :], zeroed_half
    )
    query_update = (
        adapter_scale
        * jnp.einsum(
            "fre,feo->ro",
            scatter_input,
            got_query.reshape((fetched,) + got_query.shape[2:]),
            preferred_element_type=jnp.float32,
        )
    ).astype(jnp.bfloat16)
    keyval_update = (
        adapter_scale
        * jnp.einsum(
            "fre,feo->ro",
            scatter_input,
            got_keyval.reshape((fetched,) + got_keyval.shape[2:]),
            preferred_element_type=jnp.float32,
        )
    ).astype(jnp.bfloat16)
    query_rows = (base_query + lax.optimization_barrier(query_update).astype(jnp.float32)).astype(
        jnp.bfloat16
    )
    keyval = (base_keyval + lax.optimization_barrier(keyval_update).astype(jnp.float32)).astype(
        jnp.bfloat16
    )
    att_rows = kv_cache.shape[0]
    packed = jnp.concatenate([query_rows, keyval], axis=1).reshape(tp_count, att_rows, -1)
    arrived_heads = regroup(packed)
    head_query = jnp.transpose(arrived_heads[:, :, :query_cols], (1, 0, 2)).reshape(att_rows, -1)
    head_keyval = jnp.transpose(arrived_heads[:, :, query_cols:], (1, 0, 2)).reshape(att_rows, -1)
    attended_rows = attend_block(head_query, head_keyval, kv_cache, cache_len)
    back_heads = regroup(
        jnp.transpose(attended_rows.reshape(att_rows, tp_count, query_cols), (1, 0, 2))
    )
    attended = back_heads.reshape(rows_here, query_cols)
    odown_all = got_odown.reshape((fetched,) + got_odown.shape[2:])
    output_share = jnp.einsum(
        "rc,fce->rfe", attended, odown_all, preferred_element_type=jnp.float32
    )
    adapter_output = rank_total_sum(
        jnp.sum(jnp.where(gather_hot_slots[:, :, None], output_share, 0.0), axis=1)
    ).astype(jnp.bfloat16)
    scatter_output = jnp.where(
        gather_hot_slots.T[:, :, None], adapter_output[None, :, :], zeroed_half
    )
    delta_out = (
        adapter_scale
        * jnp.einsum(
            "fre,feo->ro",
            scatter_output,
            got_oup.reshape((fetched,) + got_oup.shape[2:]),
            preferred_element_type=jnp.float32,
        )
    ).astype(jnp.bfloat16)
    summed = lax.psum_scatter(
        jnp.einsum("rc,co->or", attended, output_weight, preferred_element_type=jnp.float32).astype(
            jnp.bfloat16
        ),
        "tp",
        scatter_dimension=0,
        tiled=True,
    ).astype(jnp.float32)
    return (summed.T + lax.optimization_barrier(delta_out).astype(jnp.float32)).astype(jnp.bfloat16)


MESH = pl.DeviceIdType.MESH
VMEM_BYTES = 60 * 1024 * 1024


def remote(src, dst, send_sem, recv_sem, **where_to):
    return pltpu.make_async_remote_copy(
        src_ref=src,
        dst_ref=dst,
        send_sem=send_sem,
        recv_sem=recv_sem,
        device_id=where_to,
        device_id_type=MESH,
    )


def dot_f32(left, right):
    return jnp.dot(left, right, preferred_element_type=jnp.float32)


def dot_t(left, right):
    return lax.dot_general(
        left, right, (((1,), (1,)), ((), ())), preferred_element_type=jnp.float32
    )


def greet(owner_count, tp_count):
    my_owner = lax.axis_index("req")
    my_shard = lax.axis_index("tp")
    barrier = pltpu.get_barrier_semaphore()
    for step in range(1, tp_count):
        pl.semaphore_signal(
            barrier,
            inc=1,
            device_id={"tp": lax.rem(my_shard + step, tp_count)},
            device_id_type=MESH,
        )
    for step in range(1, owner_count):
        pl.semaphore_signal(
            barrier,
            inc=1,
            device_id={"req": lax.rem(my_owner + step, owner_count)},
            device_id_type=MESH,
        )
    return barrier


def start_loads(pairs, load_sem):
    loads = []
    for number, (source, target) in enumerate(pairs):
        load = pltpu.make_async_copy(source, target, load_sem.at[number])
        load.start()
        loads.append(load)
    return loads


class AdapterRound:
    def __init__(self, owner_count, tp_count, plan, scratch, up_scratch=None, split=0):
        self.owner_count = owner_count
        self.tp_count = tp_count
        self.named, self.pick, self.gather, self.scatter = plan
        (
            self.out_rows,
            self.in_rows,
            self.partial,
            self.out_delta,
            self.in_delta,
            self.row_sems,
            self.part_sems,
            self.delta_sems,
        ) = scratch
        self.split = split
        if split:
            (
                self.out_up,
                self.in_up,
                self.up_sems,
                self.out_low,
                self.in_low,
                self.low_sems,
            ) = up_scratch
        self.my_owner = lax.axis_index("req")
        self.my_shard = lax.axis_index("tp")
        self.sent = []

    def ahead(self, step):
        return lax.rem(self.my_owner + step, self.owner_count)

    def behind(self, step):
        return lax.rem(self.my_owner - step + self.owner_count, self.owner_count)

    def send_rows(self, rows):
        self.row_copies = {}
        for step in range(1, self.owner_count):
            holder = self.ahead(step)
            self.out_rows[step] = dot_f32(self.gather[holder], rows).astype(jnp.bfloat16)
            copy = remote(
                self.out_rows.at[step],
                self.in_rows.at[step],
                self.row_sems.at[0, step],
                self.row_sems.at[1, step],
                req=holder,
            )
            copy.start()
            self.row_copies[step] = copy
            self.sent.append(copy)
        self.in_rows[0] = dot_f32(self.gather[self.my_owner], rows).astype(jnp.bfloat16)

    def sum_rank(self, down):
        rank = down.shape[1]
        self.part_copies = {}
        for pair in range(self.owner_count // 2):
            halves = []
            for step in (2 * pair, 2 * pair + 1):
                if step:
                    self.row_copies[step].wait_recv()
                first, second = self.named[step]
                both = jnp.concatenate([down[first], down[second]], axis=0)
                share = dot_t(self.in_rows[step], both)
                halves.append(jnp.where(self.pick[step] > 0, share[:, rank:], share[:, :rank]))
            self.partial[0, pair] = jnp.concatenate(halves, axis=1)
            for step in range(1, self.tp_count):
                copy = remote(
                    self.partial.at[0, pair],
                    self.partial.at[step, pair],
                    self.part_sems.at[0, pair, step],
                    self.part_sems.at[1, pair, step],
                    tp=lax.rem(self.my_shard + step, self.tp_count),
                )
                copy.start()
                self.part_copies[pair, step] = copy
                self.sent.append(copy)

    def send_ups(self, up):
        self.up_copies = {}
        for step in range(1, self.owner_count):
            first, second = self.named[step]
            self.out_up[step] = jnp.concatenate(
                [up[first, :, : self.split], up[second, :, : self.split]], axis=0
            )
            copy = remote(
                self.out_up.at[step],
                self.in_up.at[step],
                self.up_sems.at[0, step],
                self.up_sems.at[1, step],
                req=self.behind(step),
            )
            copy.start()
            self.up_copies[step] = copy
            self.sent.append(copy)

    def send_low(self, low_rank, step):
        wide = low_rank.astype(jnp.float32)
        chosen = self.pick[step] > 0
        self.out_low[step] = jnp.concatenate(
            [jnp.where(chosen, 0.0, wide), jnp.where(chosen, wide, 0.0)], axis=1
        ).astype(jnp.bfloat16)
        copy = remote(
            self.out_low.at[step],
            self.in_low.at[step],
            self.low_sems.at[0, step],
            self.low_sems.at[1, step],
            req=self.behind(step),
        )
        copy.start()
        self.low_copies[step] = copy
        self.sent.append(copy)

    def send_delta(self, ups):
        self.delta_copies, self.low_copies = {}, {}
        for pair in range(self.owner_count // 2):
            total = self.partial[0, pair]
            for step in range(1, self.tp_count):
                self.part_copies[pair, step].wait_recv()
                total = total + self.partial[step, pair]
            total = total.astype(jnp.bfloat16)
            rank = total.shape[1] // 2
            for half in range(2):
                step = 2 * pair + half
                first, second = self.named[step]
                low_rank = total[:, half * rank : (half + 1) * rank]
                target = self.out_delta if step else self.in_delta
                skip = self.split if step else 0
                if skip:
                    self.send_low(low_rank, step)
                start = skip
                for up in ups:
                    width = up.shape[2] - skip
                    update = jnp.where(
                        self.pick[step] > 0,
                        dot_f32(low_rank, up[second, :, skip:]),
                        dot_f32(low_rank, up[first, :, skip:]),
                    )
                    target[step, :, start : start + width] = (adapter_scale * update).astype(
                        jnp.bfloat16
                    )
                    start += width
                if step:
                    copy = remote(
                        self.out_delta.at[step, :, skip:],
                        self.in_delta.at[step, :, skip:],
                        self.delta_sems.at[0, step],
                        self.delta_sems.at[1, step],
                        req=self.behind(step),
                    )
                    copy.start()
                    self.delta_copies[step] = copy
                    self.sent.append(copy)

    def add_delta(self, base):
        delta = dot_f32(self.scatter[self.my_owner], self.in_delta[0])
        for step in range(1, self.owner_count):
            if self.split:
                self.up_copies[step].wait_recv()
                self.low_copies[step].wait_recv()
                update = dot_f32(self.in_low[step], self.in_up[step])
            self.delta_copies[step].wait_recv()
            if self.split:
                self.in_delta[step, :, : self.split] = (adapter_scale * update).astype(
                    jnp.bfloat16
                )
            delta = delta + dot_f32(self.scatter[self.ahead(step)], self.in_delta[step])
        return base + delta

    def finish(self):
        for copy in self.sent:
            copy.wait_send()


def round_scratch(owner_count, tp_count, cap, width_in, rank, width_out):
    pairs = owner_count // 2
    return [
        pltpu.VMEM((owner_count, cap, width_in), jnp.bfloat16),
        pltpu.VMEM((owner_count, cap, width_in), jnp.bfloat16),
        pltpu.VMEM((tp_count, pairs, cap, 2 * rank), jnp.float32),
        pltpu.VMEM((owner_count, cap, width_out), jnp.bfloat16),
        pltpu.VMEM((owner_count, cap, width_out), jnp.bfloat16),
        pltpu.SemaphoreType.DMA((2, owner_count)),
        pltpu.SemaphoreType.DMA((2, pairs, tp_count)),
        pltpu.SemaphoreType.DMA((2, owner_count)),
    ]


ROUND_REFS = 8
UP_REFS = 6


def make_plan(owner_count, held_count, cap, adapter_ids, adapter_slot, slots, pick, gather, scatter):
    my_owner = lax.axis_index("req")
    rows = adapter_ids.shape[1]
    lookups = adapter_slot.shape[1]

    def grid(shape):
        return [lax.broadcasted_iota(jnp.int32, shape, axis) for axis in (0, 1)]

    down, across = grid((rows, rows))
    down_of, across_of = grid((lookups, lookups))
    slot_down = jnp.sum(
        jnp.where(down_of == across_of, adapter_slot[...], 0), axis=1, keepdims=True
    )
    adapter_down, _ = grid((lookups, rows))
    for asker in range(owner_count):
        same = adapter_ids[asker : asker + 1, :] == adapter_down
        slots[asker : asker + 1, :] = jnp.sum(
            jnp.where(same, slot_down, 0), axis=0, keepdims=True
        )

    def turned(row):
        return jnp.sum(jnp.where(down == across, row, 0), axis=1, keepdims=True)

    def inside(values, holder):
        return (values >= holder * held_count) & (values < (holder + 1) * held_count)

    place_down, _ = grid((cap, rows))
    _, place_across = grid((rows, cap))
    mine = slots[pl.ds(my_owner, 1), :]
    mine_down = turned(mine)
    for holder in range(owner_count):
        goes, goes_down = inside(mine, holder), inside(mine_down, holder)
        place = jnp.sum(
            jnp.where((down < across) & goes_down, 1, 0), axis=0, keepdims=True
        )
        place_of_down = jnp.sum(
            jnp.where((across < down) & goes, 1, 0), axis=1, keepdims=True
        )
        gather[holder] = jnp.where(goes & (place == place_down), 1.0, 0.0).astype(jnp.bfloat16)
        scatter[holder] = jnp.where(
            goes_down & (place_of_down == place_across), 1.0, 0.0
        ).astype(jnp.bfloat16)
    named = []
    for step in range(owner_count):
        asker = lax.rem(my_owner - step + owner_count, owner_count)
        asked = slots[pl.ds(asker, 1), :]
        asked_down = turned(asked)
        comes, comes_down = inside(asked, my_owner), inside(asked_down, my_owner)
        local = asked - my_owner * held_count
        low = jnp.min(jnp.where(comes, local, held_count - 1))
        high = jnp.max(jnp.where(comes, local, 0))
        place = jnp.sum(
            jnp.where((down < across) & comes_down, 1, 0), axis=0, keepdims=True
        )
        second = comes & (local == high) & (place == place_down)
        pick[step] = jnp.sum(jnp.where(second, 1, 0), axis=1, keepdims=True)
        named.append((low, high))
    return named


def attend_rows(cache, lengths, queries, keys, values, mixed):
    count, ctx_len, cache_width = cache.shape
    half = cache_width // 2
    per_group = QH // KVH
    score_scale = HD ** (-0.5)
    together = math.gcd(count, 16)
    own_block = lax.broadcasted_iota(jnp.int32, (QH, half), 0) // per_group == (
        lax.broadcasted_iota(jnp.int32, (QH, half), 1) // HD
    )
    head_group = lax.broadcasted_iota(jnp.int32, (QH, HD), 0) // per_group
    position = lax.broadcasted_iota(jnp.int32, (QH, ctx_len), 1)

    def body(block, carry):
        scores, news = [], []
        for inner in range(together):
            request = block * together + inner
            query = queries[request].astype(jnp.bfloat16)
            spread = jnp.where(own_block, jnp.concatenate([query] * KVH, axis=1), 0)
            score = dot_t(spread.astype(jnp.bfloat16), cache[request, :, :half]) * score_scale
            scores.append(jnp.where(position < lengths[request], score, -jnp.inf))
            news.append(
                jnp.sum(
                    query.astype(jnp.float32)
                    * keys[request].astype(jnp.bfloat16).astype(jnp.float32),
                    axis=1,
                    keepdims=True,
                )
                * score_scale
            )
        score = jnp.concatenate(scores, axis=0)
        new = jnp.concatenate(news, axis=0)
        peak = jnp.maximum(jnp.max(score, axis=1, keepdims=True), new)
        weight = jnp.exp(score - peak)
        new_weight = jnp.exp(new - peak)
        total = jnp.sum(weight, axis=1, keepdims=True) + new_weight
        prob = (weight / total).astype(jnp.bfloat16)
        new_prob = (new_weight / total).astype(jnp.bfloat16).astype(jnp.float32)
        for inner in range(together):
            request = block * together + inner
            part = slice(inner * QH, (inner + 1) * QH)
            wide = dot_f32(prob[part], cache[request, :, half:])
            result = new_prob[part] * values[request]
            for group in range(KVH):
                result = result + jnp.where(
                    head_group == group, wide[:, group * HD : (group + 1) * HD], 0.0
                )
            mixed[request] = result
        return carry

    lax.fori_loop(0, count // together, body, 0)


def layer_kernel(
    owner_count,
    tp_count,
    tokens,
    gain,
    adapter_ids,
    adapter_slot,
    turns,
    lengths,
    query_hbm,
    keyval_hbm,
    output_hbm,
    down_hbm,
    query_up_hbm,
    keyval_up_hbm,
    output_down_hbm,
    output_up_hbm,
    cache_hbm,
    out,
    *scratch,
):
    first_refs, scratch = scratch[:ROUND_REFS], scratch[ROUND_REFS:]
    second_refs, scratch = scratch[:ROUND_REFS], scratch[ROUND_REFS:]
    up_refs, scratch = scratch[:UP_REFS], scratch[UP_REFS:]
    (
        query_weight,
        keyval_weight,
        output_weight,
        down,
        wide_up,
        keyval_up,
        cache,
        load_sem,
        slots,
        pick,
        gather,
        scatter,
        squares,
        square_sems,
        normed,
        normed_sems,
        heads_out,
        heads_in,
        heads_sems,
        queries,
        keys,
        values,
        mixed,
        mixed_out,
        mixed_in,
        mixed_sems,
        attended,
        share_out,
        share_in,
        share_sems,
    ) = scratch
    my_shard = lax.axis_index("tp")
    rows, width = tokens.shape
    held_count = down.shape[0]
    cap = gather.shape[1]
    barrier = greet(owner_count, tp_count)
    loads = start_loads(
        (
            (down_hbm, down),
            (query_hbm, query_weight),
            (keyval_hbm, keyval_weight),
            (query_up_hbm, wide_up),
            (keyval_up_hbm, keyval_up),
            (cache_hbm, cache),
            (output_hbm, output_weight),
        ),
        load_sem,
    )
    late_loads = (
        pltpu.make_async_copy(output_down_hbm, down, load_sem.at[len(loads)]),
        pltpu.make_async_copy(output_up_hbm, wide_up, load_sem.at[len(loads) + 1]),
    )
    sent = []

    def swap(source_of, target, sems, steps=tuple(range(1, tp_count))):
        copies = {}
        for step in steps:
            peer = lax.rem(my_shard + step, tp_count)
            copies[step] = remote(
                source_of(step, peer), target.at[step], sems.at[0, step], sems.at[1, step], tp=peer
            )
            copies[step].start()
            sent.append(copies[step])
        return copies

    def sender(step):
        return lax.rem(my_shard - step + tp_count, tp_count)

    early = tuple(range(2, tp_count, 2))
    late = tuple(range(1, tp_count, 2))
    widened = tokens[...].astype(jnp.float32)
    own_square = jnp.sum(widened * widened, axis=1, keepdims=True)
    diagonal = lax.broadcasted_iota(jnp.int32, (rows, rows), 0) == lax.broadcasted_iota(
        jnp.int32, (rows, rows), 1
    )
    as_row = jnp.sum(jnp.where(diagonal, own_square, 0.0), axis=0, keepdims=True)
    squares[0] = jnp.broadcast_to(as_row, (8, rows))
    pl.semaphore_wait(barrier, owner_count + tp_count - 2)
    square_copies = swap(lambda step, peer: squares.at[0], squares, square_sems)
    named = make_plan(
        owner_count, held_count, cap, adapter_ids, adapter_slot, slots, pick, gather, scatter
    )
    plan = (named, pick, gather, scatter)
    first = AdapterRound(owner_count, tp_count, plan, first_refs)
    second = AdapterRound(
        owner_count, tp_count, plan, second_refs, up_refs, up_refs[0].shape[2]
    )
    total_row = squares[0]
    for step in range(1, tp_count):
        square_copies[step].wait_recv()
        total_row = total_row + squares[step]
    total = jnp.sum(jnp.where(diagonal, total_row[:1], 0.0), axis=1, keepdims=True)
    inv_rms = lax.rsqrt(total / (width * tp_count) + norm_eps)
    own = (widened * inv_rms * gain[...].astype(jnp.float32).reshape(1, width)).astype(jnp.bfloat16)
    normed[0] = own
    first.send_rows(own)
    normed_copies = swap(lambda step, peer: normed.at[0], normed, normed_sems, early)
    loads[0].wait()
    first.sum_rank(down)
    normed_copies.update(swap(lambda step, peer: normed.at[0], normed, normed_sems, late))
    late_loads[0].start()
    loads[3].wait()
    loads[4].wait()
    first.send_delta((wide_up, keyval_up))
    late_loads[1].start()
    loads[1].wait()
    loads[2].wait()
    base_query, base_keyval = 0.0, 0.0
    for step in (0, *early, *late):
        if step:
            normed_copies[step].wait_recv()
        part = pl.ds(pl.multiple_of(sender(step) * width, width), width)
        share = normed[step]
        base_query = base_query + dot_f32(share, query_weight[part, :])
        base_keyval = base_keyval + dot_f32(share, keyval_weight[part, :])
    total = first.add_delta(jnp.concatenate([base_query, base_keyval], axis=1))
    heads_out[...] = total.astype(jnp.bfloat16).reshape(heads_out.shape)
    heads_copies = swap(lambda step, peer: heads_out.at[peer], heads_in, heads_sems)
    late_loads[1].wait()
    second.send_ups(wide_up)
    heads_in[0] = heads_out[my_shard]
    cosine, sine = turns[:, :HD], turns[:, HD:]

    def rotated(vector):
        half = HD // 2
        swapped = jnp.concatenate([vector[:, half:], vector[:, :half]], axis=1)
        return vector * cosine + swapped * sine

    query_cols = query_weight.shape[1]
    per_group = QH // KVH
    per_shard = query_cols // HD
    keyval_shard = keyval_weight.shape[1] // HD
    for step in range(1, tp_count):
        heads_copies[step].wait_recv()
    for shard in range(tp_count):
        slot = lax.rem(my_shard - shard + tp_count, tp_count)
        block = heads_in[slot].astype(jnp.float32)
        for head in range(per_shard):
            queries[:, shard * per_shard + head, :] = rotated(
                block[:, head * HD : (head + 1) * HD]
            )
        for head in range(keyval_shard):
            number = shard * keyval_shard + head
            start = query_cols + head * HD
            vector = block[:, start : start + HD]
            target, vector = (keys, rotated(vector)) if number < KVH else (values, vector)
            for copy_of in range(per_group):
                target[:, (number % KVH) * per_group + copy_of, :] = vector
    loads[5].wait()
    attend_rows(cache, lengths, queries, keys, values, mixed)
    for shard in range(tp_count):
        for head in range(per_shard):
            mixed_out[shard, :, head * HD : (head + 1) * HD] = mixed[
                :, shard * per_shard + head, :
            ].astype(jnp.bfloat16)
    mixed_copies = swap(lambda step, peer: mixed_out.at[peer], mixed_in, mixed_sems)
    mixed_in[0] = mixed_out[my_shard]
    att_rows = mixed_in.shape[1]
    for step in range(tp_count):
        if step:
            mixed_copies[step].wait_recv()
        attended[pl.ds(pl.multiple_of(sender(step) * att_rows, att_rows), att_rows), :] = mixed_in[
            step
        ]
    own = attended[...]
    second.send_rows(own)
    loads[6].wait()
    out_width = out.shape[1]

    def output_share(peer):
        return dot_f32(
            own, output_weight[:, pl.ds(pl.multiple_of(peer * out_width, out_width), out_width)]
        )

    def staged_share(step, peer):
        share_out[step] = output_share(peer).astype(jnp.bfloat16)
        return share_out.at[step]

    share_copies = swap(staged_share, share_in, share_sems, early)
    for step in late:
        staged_share(step, lax.rem(my_shard + step, tp_count))
    base = output_share(my_shard)
    late_loads[0].wait()
    second.sum_rank(down)
    share_copies.update(
        swap(lambda step, peer: share_out.at[step], share_in, share_sems, late)
    )
    second.send_delta((wide_up,))
    for step in range(1, tp_count):
        share_copies[step].wait_recv()
        base = base + share_in[step].astype(jnp.float32)
    out[...] = second.add_delta(base).astype(jnp.bfloat16)
    for copy in sent:
        copy.wait_send()
    first.finish()
    second.finish()


def turn_table(lengths):
    half_dim = HD // 2
    frequency = rope_theta ** (-(2.0 * jnp.arange(half_dim, dtype=jnp.float32)) / HD)
    angles = lengths.astype(jnp.float32)[:, None] * frequency
    cosine, sine = jnp.cos(angles), jnp.sin(angles)
    return jnp.concatenate([cosine, cosine, -sine, sine], axis=1)


VMEM_SPEC = pl.BlockSpec(memory_space=pltpu.VMEM)
SMEM_SPEC = pl.BlockSpec(memory_space=pltpu.SMEM)
HBM_SPEC = pl.BlockSpec(memory_space=pl.ANY)


def routed_device(
    tokens,
    norm_gain,
    query_weight,
    keyval_weight,
    output_weight,
    projection_down_weight,
    query_up_weight,
    keyval_up_weight,
    output_down_weight,
    output_up_weight,
    adapter_ids,
    adapter_slot,
    kv_cache,
    cache_len,
):
    owner_count = lax.axis_size("req")
    tp_count = lax.axis_size("tp")
    held_count, width, rank = projection_down_weight.shape
    rows = tokens.shape[0]
    cap = FETCH_OWN * rows // owner_count
    att_rows = kv_cache.shape[0]
    query_cols = query_weight.shape[1]
    head_cols = query_cols + keyval_weight.shape[1]
    out_cols = output_up_weight.shape[2]
    sems = pltpu.SemaphoreType.DMA
    vmem = pltpu.VMEM
    return pl.pallas_call(
        functools.partial(layer_kernel, owner_count, tp_count),
        out_shape=jax.ShapeDtypeStruct((rows, out_cols), jnp.bfloat16),
        in_specs=[VMEM_SPEC] * 5 + [SMEM_SPEC] + [HBM_SPEC] * 9,
        out_specs=VMEM_SPEC,
        scratch_shapes=round_scratch(owner_count, tp_count, cap, width, rank, head_cols)
        + round_scratch(owner_count, tp_count, cap, query_cols, rank, out_cols)
        + [
            vmem((owner_count, 2 * rank, out_cols // 2), jnp.bfloat16),
            vmem((owner_count, 2 * rank, out_cols // 2), jnp.bfloat16),
            sems((2, owner_count)),
            vmem((owner_count, cap, 2 * rank), jnp.bfloat16),
            vmem((owner_count, cap, 2 * rank), jnp.bfloat16),
            sems((2, owner_count)),
        ]
        + [
            vmem(query_weight.shape, jnp.bfloat16),
            vmem(keyval_weight.shape, jnp.bfloat16),
            vmem(output_weight.shape, jnp.bfloat16),
            vmem((held_count, rank, width), jnp.bfloat16),
            vmem(query_up_weight.shape, jnp.bfloat16),
            vmem(keyval_up_weight.shape, jnp.bfloat16),
            vmem(kv_cache.shape, jnp.bfloat16),
            sems((9,)),
            vmem((owner_count, rows), jnp.int32),
            vmem((owner_count, cap, 1), jnp.int32),
            vmem((owner_count, cap, rows), jnp.bfloat16),
            vmem((owner_count, rows, cap), jnp.bfloat16),
            vmem((tp_count, 8, rows), jnp.float32),
            sems((2, tp_count)),
            vmem((tp_count, rows, width), jnp.bfloat16),
            sems((2, tp_count)),
            vmem((tp_count, att_rows, head_cols), jnp.bfloat16),
            vmem((tp_count, att_rows, head_cols), jnp.bfloat16),
            sems((2, tp_count)),
            vmem((att_rows, QH, HD), jnp.float32),
            vmem((att_rows, QH, HD), jnp.float32),
            vmem((att_rows, QH, HD), jnp.float32),
            vmem((att_rows, QH, HD), jnp.float32),
            vmem((tp_count, att_rows, query_cols), jnp.bfloat16),
            vmem((tp_count, att_rows, query_cols), jnp.bfloat16),
            sems((2, tp_count)),
            vmem((rows, query_cols), jnp.bfloat16),
            vmem((tp_count, rows, out_cols), jnp.bfloat16),
            vmem((tp_count, rows, out_cols), jnp.bfloat16),
            sems((2, tp_count)),
        ],
        compiler_params=pltpu.CompilerParams(
            collective_id=1, has_side_effects=True, vmem_limit_bytes=VMEM_BYTES
        ),
    )(
        tokens,
        norm_gain,
        adapter_ids.reshape(owner_count, rows),
        adapter_slot[None, :],
        turn_table(cache_len),
        cache_len,
        query_weight,
        keyval_weight,
        output_weight,
        jnp.swapaxes(projection_down_weight, 1, 2),
        query_up_weight,
        keyval_up_weight,
        jnp.swapaxes(output_down_weight, 1, 2),
        output_up_weight,
        kv_cache,
    )


def fits_kernels(mesh):
    tp_count, owner_count = mesh.shape["tp"], mesh.shape["req"]
    return (2 * KVH * HD // tp_count) % HD == 0 and tp_count <= KVH and owner_count % 2 == 0


def solution(mesh):
    in_specs = (
        P(("group", "req"), "tp"),
        P("tp"),
        P(None, "tp"),
        P(None, "tp"),
        P("tp", None),
        P(("group", "req"), "tp", None),
        P(("group", "req"), None, "tp"),
        P(("group", "req"), None, "tp"),
        P(("group", "req"), "tp", None),
        P(("group", "req"), None, "tp"),
        P("group"),
        P("group"),
        P(("group", "req", "tp"), None, None),
        P(("group", "req", "tp")),
    )
    out_specs = P(("group", "req"), "tp")
    return jax.shard_map(
        routed_device if fits_kernels(mesh) else per_device,
        mesh=mesh, in_specs=in_specs, out_specs=out_specs, check_vma=False
    )
```

```python
import functools
import math

import jax
import jax.numpy as jnp
from jax import lax
from jax.experimental import pallas as pl
from jax.experimental.pallas import tpu as pltpu
from jax.sharding import PartitionSpec as P

QH = 32
KVH = 4
HD = 128
FETCH_OWN = 2


norm_eps = 1e-05
adapter_scale = 0.5
rope_theta = 500000.0


def rotate(vector, position):
    half_dim = vector.shape[-1] // 2
    frequency = rope_theta ** (-(2.0 * jnp.arange(half_dim, dtype=jnp.float32)) / vector.shape[-1])
    angles = position * frequency
    cosine = jnp.cos(angles)
    sine_part = jnp.sin(angles)
    first_half = vector[..., :half_dim]
    second = vector[..., half_dim:]
    return jnp.concatenate(
        [first_half * cosine - second * sine_part, second * cosine + first_half * sine_part],
        axis=-1,
    )


def attend_block(query_rows, keyval, cache_rows, lengths):
    req_count = cache_rows.shape[0]
    ctx_len = cache_rows.shape[1]
    per_group = QH // KVH
    score_scale = HD ** (-0.5)
    position = lengths.astype(jnp.float32)[:, None, None]
    rot_query = rotate(query_rows.reshape(req_count, QH, HD).astype(jnp.float32), position).astype(
        jnp.bfloat16
    )
    rot_query = rot_query.reshape(req_count, KVH, per_group, HD)
    rot_key = rotate(
        keyval[:, : KVH * HD].reshape(req_count, KVH, HD).astype(jnp.float32), position
    ).astype(jnp.bfloat16)
    new_value = keyval[:, KVH * HD :].reshape(req_count, KVH, HD)
    old_keys = cache_rows[:, :, : KVH * HD].reshape(req_count, ctx_len, KVH, HD)
    old_values = cache_rows[:, :, KVH * HD :].reshape(req_count, ctx_len, KVH, HD)
    old_score = (
        jnp.einsum("akgd,apkd->akgp", rot_query, old_keys, preferred_element_type=jnp.float32)
        * score_scale
    )
    new_score = (
        jnp.einsum("akgd,akd->akg", rot_query, rot_key, preferred_element_type=jnp.float32)
        * score_scale
    )
    is_live = jnp.arange(ctx_len)[None, :] < lengths[:, None]
    old_score = jnp.where(is_live[:, None, None, :], old_score, -jnp.inf)
    peak_score = jnp.maximum(jnp.max(old_score, axis=-1), new_score)
    old_weight = jnp.exp(old_score - peak_score[..., None])
    new_weight = jnp.exp(new_score - peak_score)
    denominator = jnp.sum(old_weight, axis=-1) + new_weight
    old_prob = (old_weight / denominator[..., None]).astype(jnp.bfloat16)
    new_prob = (new_weight / denominator).astype(jnp.bfloat16)
    mixture = jnp.einsum(
        "akgp,apkd->akgd", old_prob, old_values, preferred_element_type=jnp.float32
    )
    mixture = (
        mixture
        + new_prob.astype(jnp.float32)[..., None] * new_value.astype(jnp.float32)[:, :, None, :]
    )
    return mixture.reshape(req_count, QH * HD).astype(jnp.bfloat16)


def route_plan(adapter_ids, adapter_slot, owner_count, held_count):
    lookup = jnp.arange(adapter_slot.shape[0], dtype=jnp.int32)
    matches = adapter_ids[:, None] == lookup[None, :]
    slot_of = jnp.sum(jnp.where(matches, adapter_slot[None, :], 0), axis=1).reshape(owner_count, -1)
    holder = slot_of // held_count
    local_index = slot_of % held_count
    holder_hot = holder[:, :, None] == jnp.arange(owner_count, dtype=jnp.int32)[None, None, :]
    local_hot = local_index[:, :, None] == jnp.arange(held_count, dtype=jnp.int32)[None, None, :]
    both_hot = holder_hot[:, :, :, None] & local_hot[:, :, None, :]
    used_any = jnp.any(both_hot, axis=1)
    rank_in = jnp.cumsum(used_any.astype(jnp.int32), axis=2) - 1
    pick_ids = jnp.arange(FETCH_OWN, dtype=jnp.int32)
    chosen = used_any[..., None] & (rank_in[..., None] == pick_ids)
    wanted = jnp.sum(
        jnp.where(chosen, jnp.arange(held_count, dtype=jnp.int32)[None, None, :, None], 0), axis=2
    )
    row_pick = jnp.sum(jnp.where(both_hot, rank_in[:, None, :, :], 0), axis=(2, 3))
    row_place = (
        jnp.sum(jnp.where(holder_hot, jnp.cumsum(holder_hot.astype(jnp.int32), axis=1), 0), axis=2)
        - 1
    )
    return (holder, row_pick, row_place, wanted)


def rank_total_sum(partial_value):
    return lax.psum(partial_value, "tp")


def regroup(pieces):
    return lax.all_to_all(pieces, "tp", split_axis=0, concat_axis=0, tiled=True)


def per_device(
    tokens,
    norm_gain,
    query_weight,
    keyval_weight,
    output_weight,
    projection_down_weight,
    query_up_weight,
    keyval_up_weight,
    output_down_weight,
    output_up_weight,
    adapter_ids,
    adapter_slot,
    kv_cache,
    cache_len,
):
    owner_count = lax.axis_size("req")
    tp_count = lax.axis_size("tp")
    held_count = projection_down_weight.shape[0]
    my_owner = lax.axis_index("req")
    my_shard = lax.axis_index("tp")
    rows_here = tokens.shape[0]
    shard_width = tokens.shape[1]
    zeroed_half = jnp.zeros((), jnp.bfloat16)
    gathered, gain_whole = (
        lax.all_gather(tokens, "tp", axis=1, tiled=True),
        lax.all_gather(norm_gain, "tp", axis=0, tiled=True),
    )
    widened = gathered.astype(jnp.float32)
    inv_rms = lax.rsqrt(jnp.mean(widened * widened, axis=1, keepdims=True) + norm_eps)
    normed = (widened * inv_rms * gain_whole.astype(jnp.float32)).astype(jnp.bfloat16)
    normalized_share = lax.dynamic_slice_in_dim(normed, my_shard * shard_width, shard_width, 1)
    holder, row_pick, row_place, wanted = route_plan(
        adapter_ids, adapter_slot, owner_count, held_count
    )
    my_holder = lax.dynamic_index_in_dim(holder, my_owner, 0, keepdims=False)
    my_pick = lax.dynamic_index_in_dim(row_pick, my_owner, 0, keepdims=False)
    asked_for = lax.dynamic_index_in_dim(wanted, my_owner, 1, keepdims=False)

    def held_blocks(lookup_table):
        taken_rows = jnp.take(lookup_table, asked_for.reshape(-1), axis=0)
        return taken_rows.reshape(asked_for.shape + lookup_table.shape[1:])

    base_query = jnp.dot(normed, query_weight, preferred_element_type=jnp.float32)
    base_keyval = jnp.dot(normed, keyval_weight, preferred_element_type=jnp.float32)
    query_cols = query_weight.shape[1]
    got_down, got_query, got_keyval, got_odown, got_oup = (
        lax.all_to_all(
            held_blocks(projection_down_weight), "req", split_axis=0, concat_axis=0, tiled=True
        ),
        lax.all_to_all(
            held_blocks(query_up_weight), "req", split_axis=0, concat_axis=0, tiled=True
        ),
        lax.all_to_all(
            held_blocks(keyval_up_weight), "req", split_axis=0, concat_axis=0, tiled=True
        ),
        lax.all_to_all(
            held_blocks(output_down_weight), "req", split_axis=0, concat_axis=0, tiled=True
        ),
        lax.all_to_all(
            held_blocks(output_up_weight), "req", split_axis=0, concat_axis=0, tiled=True
        ),
    )
    fetched = owner_count * FETCH_OWN
    fetch_index = my_holder * FETCH_OWN + my_pick
    gather_hot_slots = fetch_index[:, None] == jnp.arange(fetched, dtype=jnp.int32)[None, :]
    down_matrix_table = got_down.reshape((fetched,) + got_down.shape[2:])
    adapter_share = jnp.einsum(
        "jg,vgi->jvi", normalized_share, down_matrix_table, preferred_element_type=jnp.float32
    )
    adapter_input = rank_total_sum(
        jnp.sum(jnp.where(gather_hot_slots[:, :, None], adapter_share, 0.0), axis=1)
    ).astype(jnp.bfloat16)
    scatter_input = jnp.where(
        gather_hot_slots.T[:, :, None], adapter_input[None, :, :], zeroed_half
    )
    query_update = (
        adapter_scale
        * jnp.einsum(
            "fre,feo->ro",
            scatter_input,
            got_query.reshape((fetched,) + got_query.shape[2:]),
            preferred_element_type=jnp.float32,
        )
    ).astype(jnp.bfloat16)
    keyval_update = (
        adapter_scale
        * jnp.einsum(
            "fre,feo->ro",
            scatter_input,
            got_keyval.reshape((fetched,) + got_keyval.shape[2:]),
            preferred_element_type=jnp.float32,
        )
    ).astype(jnp.bfloat16)
    query_rows = (base_query + lax.optimization_barrier(query_update).astype(jnp.float32)).astype(
        jnp.bfloat16
    )
    keyval = (base_keyval + lax.optimization_barrier(keyval_update).astype(jnp.float32)).astype(
        jnp.bfloat16
    )
    att_rows = kv_cache.shape[0]
    packed = jnp.concatenate([query_rows, keyval], axis=1).reshape(tp_count, att_rows, -1)
    arrived_heads = regroup(packed)
    head_query = jnp.transpose(arrived_heads[:, :, :query_cols], (1, 0, 2)).reshape(att_rows, -1)
    head_keyval = jnp.transpose(arrived_heads[:, :, query_cols:], (1, 0, 2)).reshape(att_rows, -1)
    attended_rows = attend_block(head_query, head_keyval, kv_cache, cache_len)
    back_heads = regroup(
        jnp.transpose(attended_rows.reshape(att_rows, tp_count, query_cols), (1, 0, 2))
    )
    attended = back_heads.reshape(rows_here, query_cols)
    odown_all = got_odown.reshape((fetched,) + got_odown.shape[2:])
    output_share = jnp.einsum(
        "rc,fce->rfe", attended, odown_all, preferred_element_type=jnp.float32
    )
    adapter_output = rank_total_sum(
        jnp.sum(jnp.where(gather_hot_slots[:, :, None], output_share, 0.0), axis=1)
    ).astype(jnp.bfloat16)
    scatter_output = jnp.where(
        gather_hot_slots.T[:, :, None], adapter_output[None, :, :], zeroed_half
    )
    delta_out = (
        adapter_scale
        * jnp.einsum(
            "fre,feo->ro",
            scatter_output,
            got_oup.reshape((fetched,) + got_oup.shape[2:]),
            preferred_element_type=jnp.float32,
        )
    ).astype(jnp.bfloat16)
    summed = lax.psum_scatter(
        jnp.einsum("rc,co->or", attended, output_weight, preferred_element_type=jnp.float32).astype(
            jnp.bfloat16
        ),
        "tp",
        scatter_dimension=0,
        tiled=True,
    ).astype(jnp.float32)
    return (summed.T + lax.optimization_barrier(delta_out).astype(jnp.float32)).astype(jnp.bfloat16)


MESH = pl.DeviceIdType.MESH
VMEM_BYTES = 60 * 1024 * 1024


def remote(src, dst, send_sem, recv_sem, **where_to):
    return pltpu.make_async_remote_copy(
        src_ref=src,
        dst_ref=dst,
        send_sem=send_sem,
        recv_sem=recv_sem,
        device_id=where_to,
        device_id_type=MESH,
    )


def dot_f32(left, right):
    return jnp.dot(left, right, preferred_element_type=jnp.float32)


def dot_t(left, right):
    return lax.dot_general(
        left, right, (((1,), (1,)), ((), ())), preferred_element_type=jnp.float32
    )


def greet(owner_count, tp_count):
    my_owner = lax.axis_index("req")
    my_shard = lax.axis_index("tp")
    barrier = pltpu.get_barrier_semaphore()
    for step in range(1, tp_count):
        pl.semaphore_signal(
            barrier,
            inc=1,
            device_id={"tp": lax.rem(my_shard + step, tp_count)},
            device_id_type=MESH,
        )
    for step in range(1, owner_count):
        pl.semaphore_signal(
            barrier,
            inc=1,
            device_id={"req": lax.rem(my_owner + step, owner_count)},
            device_id_type=MESH,
        )
    return barrier


def start_loads(pairs, load_sem):
    loads = []
    for number, (source, target) in enumerate(pairs):
        load = pltpu.make_async_copy(source, target, load_sem.at[number])
        load.start()
        loads.append(load)
    return loads


class AdapterRound:
    def __init__(self, owner_count, tp_count, plan, scratch, up_scratch=None, split=0):
        self.owner_count = owner_count
        self.tp_count = tp_count
        self.named, self.pick, self.gather, self.scatter = plan
        (
            self.out_rows,
            self.in_rows,
            self.partial,
            self.out_delta,
            self.in_delta,
            self.row_sems,
            self.part_sems,
            self.delta_sems,
        ) = scratch
        self.split = split
        if split:
            (
                self.out_up,
                self.in_up,
                self.up_sems,
                self.out_low,
                self.in_low,
                self.low_sems,
            ) = up_scratch
        self.my_owner = lax.axis_index("req")
        self.my_shard = lax.axis_index("tp")
        self.sent = []

    def ahead(self, step):
        return lax.rem(self.my_owner + step, self.owner_count)

    def behind(self, step):
        return lax.rem(self.my_owner - step + self.owner_count, self.owner_count)

    def send_rows(self, rows):
        self.row_copies = {}
        for step in range(1, self.owner_count):
            holder = self.ahead(step)
            self.out_rows[step] = dot_f32(self.gather[holder], rows).astype(jnp.bfloat16)
            copy = remote(
                self.out_rows.at[step],
                self.in_rows.at[step],
                self.row_sems.at[0, step],
                self.row_sems.at[1, step],
                req=holder,
            )
            copy.start()
            self.row_copies[step] = copy
            self.sent.append(copy)
        self.in_rows[0] = dot_f32(self.gather[self.my_owner], rows).astype(jnp.bfloat16)

    def sum_rank(self, down):
        rank = down.shape[1]
        self.part_copies = {}
        for pair in range(self.owner_count // 2):
            halves = []
            for step in (2 * pair, 2 * pair + 1):
                if step:
                    self.row_copies[step].wait_recv()
                first, second = self.named[step]
                both = jnp.concatenate([down[first], down[second]], axis=0)
                share = dot_t(self.in_rows[step], both)
                halves.append(jnp.where(self.pick[step] > 0, share[:, rank:], share[:, :rank]))
            self.partial[0, pair] = jnp.concatenate(halves, axis=1)
            for step in range(1, self.tp_count):
                copy = remote(
                    self.partial.at[0, pair],
                    self.partial.at[step, pair],
                    self.part_sems.at[0, pair, step],
                    self.part_sems.at[1, pair, step],
                    tp=lax.rem(self.my_shard + step, self.tp_count),
                )
                copy.start()
                self.part_copies[pair, step] = copy
                self.sent.append(copy)

    def send_ups(self, up):
        self.up_copies = {}
        for step in range(1, self.owner_count):
            first, second = self.named[step]
            self.out_up[step] = jnp.concatenate(
                [up[first, :, : self.split], up[second, :, : self.split]], axis=0
            )
            copy = remote(
                self.out_up.at[step],
                self.in_up.at[step],
                self.up_sems.at[0, step],
                self.up_sems.at[1, step],
                req=self.behind(step),
            )
            copy.start()
            self.up_copies[step] = copy
            self.sent.append(copy)

    def send_low(self, low_rank, step):
        wide = low_rank.astype(jnp.float32)
        chosen = self.pick[step] > 0
        self.out_low[step] = jnp.concatenate(
            [jnp.where(chosen, 0.0, wide), jnp.where(chosen, wide, 0.0)], axis=1
        ).astype(jnp.bfloat16)
        copy = remote(
            self.out_low.at[step],
            self.in_low.at[step],
            self.low_sems.at[0, step],
            self.low_sems.at[1, step],
            req=self.behind(step),
        )
        copy.start()
        self.low_copies[step] = copy
        self.sent.append(copy)

    def send_delta(self, ups):
        self.delta_copies, self.low_copies = {}, {}
        for pair in range(self.owner_count // 2):
            total = self.partial[0, pair]
            for step in range(1, self.tp_count):
                self.part_copies[pair, step].wait_recv()
                total = total + self.partial[step, pair]
            total = total.astype(jnp.bfloat16)
            rank = total.shape[1] // 2
            for half in range(2):
                step = 2 * pair + half
                first, second = self.named[step]
                low_rank = total[:, half * rank : (half + 1) * rank]
                target = self.out_delta if step else self.in_delta
                skip = self.split if step else 0
                if skip:
                    self.send_low(low_rank, step)
                start = skip
                for up in ups:
                    width = up.shape[2] - skip
                    update = jnp.where(
                        self.pick[step] > 0,
                        dot_f32(low_rank, up[second, :, skip:]),
                        dot_f32(low_rank, up[first, :, skip:]),
                    )
                    target[step, :, start : start + width] = (adapter_scale * update).astype(
                        jnp.bfloat16
                    )
                    start += width
                if step:
                    copy = remote(
                        self.out_delta.at[step, :, skip:],
                        self.in_delta.at[step, :, skip:],
                        self.delta_sems.at[0, step],
                        self.delta_sems.at[1, step],
                        req=self.behind(step),
                    )
                    copy.start()
                    self.delta_copies[step] = copy
                    self.sent.append(copy)

    def add_delta(self, base):
        delta = dot_f32(self.scatter[self.my_owner], self.in_delta[0])
        for step in range(1, self.owner_count):
            if self.split:
                self.up_copies[step].wait_recv()
                self.low_copies[step].wait_recv()
                update = dot_f32(self.in_low[step], self.in_up[step])
            self.delta_copies[step].wait_recv()
            if self.split:
                self.in_delta[step, :, : self.split] = (adapter_scale * update).astype(
                    jnp.bfloat16
                )
            delta = delta + dot_f32(self.scatter[self.ahead(step)], self.in_delta[step])
        return base + delta

    def finish(self):
        for copy in self.sent:
            copy.wait_send()


def round_scratch(owner_count, tp_count, cap, width_in, rank, width_out):
    pairs = owner_count // 2
    return [
        pltpu.VMEM((owner_count, cap, width_in), jnp.bfloat16),
        pltpu.VMEM((owner_count, cap, width_in), jnp.bfloat16),
        pltpu.VMEM((tp_count, pairs, cap, 2 * rank), jnp.float32),
        pltpu.VMEM((owner_count, cap, width_out), jnp.bfloat16),
        pltpu.VMEM((owner_count, cap, width_out), jnp.bfloat16),
        pltpu.SemaphoreType.DMA((2, owner_count)),
        pltpu.SemaphoreType.DMA((2, pairs, tp_count)),
        pltpu.SemaphoreType.DMA((2, owner_count)),
    ]


ROUND_REFS = 8
UP_REFS = 6


def make_plan(owner_count, held_count, cap, adapter_ids, adapter_slot, slots, pick, gather, scatter):
    my_owner = lax.axis_index("req")
    rows = adapter_ids.shape[1]
    lookups = adapter_slot.shape[1]

    def grid(shape):
        return [lax.broadcasted_iota(jnp.int32, shape, axis) for axis in (0, 1)]

    down, across = grid((rows, rows))
    down_of, across_of = grid((lookups, lookups))
    slot_down = jnp.sum(
        jnp.where(down_of == across_of, adapter_slot[...], 0), axis=1, keepdims=True
    )
    adapter_down, _ = grid((lookups, rows))
    for asker in range(owner_count):
        same = adapter_ids[asker : asker + 1, :] == adapter_down
        slots[asker : asker + 1, :] = jnp.sum(
            jnp.where(same, slot_down, 0), axis=0, keepdims=True
        )

    def turned(row):
        return jnp.sum(jnp.where(down == across, row, 0), axis=1, keepdims=True)

    def inside(values, holder):
        return (values >= holder * held_count) & (values < (holder + 1) * held_count)

    place_down, _ = grid((cap, rows))
    _, place_across = grid((rows, cap))
    mine = slots[pl.ds(my_owner, 1), :]
    mine_down = turned(mine)
    for holder in range(owner_count):
        goes, goes_down = inside(mine, holder), inside(mine_down, holder)
        place = jnp.sum(
            jnp.where((down < across) & goes_down, 1, 0), axis=0, keepdims=True
        )
        place_of_down = jnp.sum(
            jnp.where((across < down) & goes, 1, 0), axis=1, keepdims=True
        )
        gather[holder] = jnp.where(goes & (place == place_down), 1.0, 0.0).astype(jnp.bfloat16)
        scatter[holder] = jnp.where(
            goes_down & (place_of_down == place_across), 1.0, 0.0
        ).astype(jnp.bfloat16)
    named = []
    for step in range(owner_count):
        asker = lax.rem(my_owner - step + owner_count, owner_count)
        asked = slots[pl.ds(asker, 1), :]
        asked_down = turned(asked)
        comes, comes_down = inside(asked, my_owner), inside(asked_down, my_owner)
        local = asked - my_owner * held_count
        low = jnp.min(jnp.where(comes, local, held_count - 1))
        high = jnp.max(jnp.where(comes, local, 0))
        place = jnp.sum(
            jnp.where((down < across) & comes_down, 1, 0), axis=0, keepdims=True
        )
        second = comes & (local == high) & (place == place_down)
        pick[step] = jnp.sum(jnp.where(second, 1, 0), axis=1, keepdims=True)
        named.append((low, high))
    return named


def attend_rows(cache, lengths, queries, keys, values, mixed):
    count, ctx_len, cache_width = cache.shape
    half = cache_width // 2
    per_group = QH // KVH
    score_scale = HD ** (-0.5)
    together = math.gcd(count, 32)
    own_block = lax.broadcasted_iota(jnp.int32, (QH, half), 0) // per_group == (
        lax.broadcasted_iota(jnp.int32, (QH, half), 1) // HD
    )
    head_group = lax.broadcasted_iota(jnp.int32, (QH, HD), 0) // per_group
    position = lax.broadcasted_iota(jnp.int32, (QH, ctx_len), 1)

    def body(block, carry):
        scores, news = [], []
        for inner in range(together):
            request = block * together + inner
            query = queries[request].astype(jnp.bfloat16)
            spread = jnp.where(own_block, jnp.concatenate([query] * KVH, axis=1), 0)
            score = dot_t(spread.astype(jnp.bfloat16), cache[request, :, :half]) * score_scale
            scores.append(jnp.where(position < lengths[request], score, -jnp.inf))
            news.append(
                jnp.sum(
                    query.astype(jnp.float32)
                    * keys[request].astype(jnp.bfloat16).astype(jnp.float32),
                    axis=1,
                    keepdims=True,
                )
                * score_scale
            )
        score = jnp.concatenate(scores, axis=0)
        new = jnp.concatenate(news, axis=0)
        peak = jnp.maximum(jnp.max(score, axis=1, keepdims=True), new)
        weight = jnp.exp(score - peak)
        new_weight = jnp.exp(new - peak)
        total = jnp.sum(weight, axis=1, keepdims=True) + new_weight
        prob = (weight / total).astype(jnp.bfloat16)
        new_prob = (new_weight / total).astype(jnp.bfloat16).astype(jnp.float32)
        for inner in range(together):
            request = block * together + inner
            part = slice(inner * QH, (inner + 1) * QH)
            wide = dot_f32(prob[part], cache[request, :, half:])
            result = new_prob[part] * values[request]
            for group in range(KVH):
                result = result + jnp.where(
                    head_group == group, wide[:, group * HD : (group + 1) * HD], 0.0
                )
            mixed[request] = result
        return carry

    lax.fori_loop(0, count // together, body, 0)


def layer_kernel(
    owner_count,
    tp_count,
    tokens,
    gain,
    adapter_ids,
    adapter_slot,
    cosines,
    sines,
    lengths,
    query_hbm,
    keyval_hbm,
    output_hbm,
    down_hbm,
    query_up_hbm,
    keyval_up_hbm,
    output_down_hbm,
    output_up_hbm,
    cache_hbm,
    out,
    *scratch,
):
    first_refs, scratch = scratch[:ROUND_REFS], scratch[ROUND_REFS:]
    second_refs, scratch = scratch[:ROUND_REFS], scratch[ROUND_REFS:]
    up_refs, scratch = scratch[:UP_REFS], scratch[UP_REFS:]
    (
        query_weight,
        keyval_weight,
        output_weight,
        down,
        wide_up,
        keyval_up,
        cache,
        load_sem,
        slots,
        pick,
        gather,
        scatter,
        squares,
        square_sems,
        normed,
        normed_sems,
        heads_out,
        heads_in,
        heads_sems,
        queries,
        keys,
        values,
        mixed,
        mixed_out,
        mixed_in,
        mixed_sems,
        attended,
        share_out,
        share_in,
        share_sems,
    ) = scratch
    my_shard = lax.axis_index("tp")
    rows, width = tokens.shape
    held_count = down.shape[0]
    cap = gather.shape[1]
    barrier = greet(owner_count, tp_count)
    loads = start_loads(
        (
            (down_hbm, down),
            (query_hbm, query_weight),
            (keyval_hbm, keyval_weight),
            (query_up_hbm, wide_up),
            (keyval_up_hbm, keyval_up),
            (cache_hbm, cache),
            (output_hbm, output_weight),
        ),
        load_sem,
    )
    late_loads = (
        pltpu.make_async_copy(output_down_hbm, down, load_sem.at[len(loads)]),
        pltpu.make_async_copy(output_up_hbm, wide_up, load_sem.at[len(loads) + 1]),
    )
    sent = []

    def swap(source_of, target, sems, steps=tuple(range(1, tp_count))):
        copies = {}
        for step in steps:
            peer = lax.rem(my_shard + step, tp_count)
            copies[step] = remote(
                source_of(step, peer), target.at[step], sems.at[0, step], sems.at[1, step], tp=peer
            )
            copies[step].start()
            sent.append(copies[step])
        return copies

    def sender(step):
        return lax.rem(my_shard - step + tp_count, tp_count)

    early = tuple(range(2, tp_count, 2))
    late = tuple(range(1, tp_count, 2))
    widened = tokens[...].astype(jnp.float32)
    own_square = jnp.sum(widened * widened, axis=1, keepdims=True)
    diagonal = lax.broadcasted_iota(jnp.int32, (rows, rows), 0) == lax.broadcasted_iota(
        jnp.int32, (rows, rows), 1
    )
    as_row = jnp.sum(jnp.where(diagonal, own_square, 0.0), axis=0, keepdims=True)
    squares[0] = jnp.broadcast_to(as_row, (8, rows))
    pl.semaphore_wait(barrier, owner_count + tp_count - 2)
    square_copies = swap(lambda step, peer: squares.at[0], squares, square_sems)
    named = make_plan(
        owner_count, held_count, cap, adapter_ids, adapter_slot, slots, pick, gather, scatter
    )
    plan = (named, pick, gather, scatter)
    first = AdapterRound(owner_count, tp_count, plan, first_refs)
    second = AdapterRound(
        owner_count, tp_count, plan, second_refs, up_refs, up_refs[0].shape[2]
    )
    total_row = squares[0]
    for step in range(1, tp_count):
        square_copies[step].wait_recv()
        total_row = total_row + squares[step]
    total = jnp.sum(jnp.where(diagonal, total_row[:1], 0.0), axis=1, keepdims=True)
    inv_rms = lax.rsqrt(total / (width * tp_count) + norm_eps)
    own = (widened * inv_rms * gain[...].astype(jnp.float32).reshape(1, width)).astype(jnp.bfloat16)
    normed[0] = own
    first.send_rows(own)
    normed_copies = swap(lambda step, peer: normed.at[0], normed, normed_sems, early)
    loads[0].wait()
    first.sum_rank(down)
    normed_copies.update(swap(lambda step, peer: normed.at[0], normed, normed_sems, late))
    late_loads[0].start()
    loads[3].wait()
    loads[4].wait()
    first.send_delta((wide_up, keyval_up))
    late_loads[1].start()
    loads[1].wait()
    loads[2].wait()
    base_query, base_keyval = 0.0, 0.0
    for step in (0, *early, *late):
        if step:
            normed_copies[step].wait_recv()
        part = pl.ds(pl.multiple_of(sender(step) * width, width), width)
        share = normed[step]
        base_query = base_query + dot_f32(share, query_weight[part, :])
        base_keyval = base_keyval + dot_f32(share, keyval_weight[part, :])
    total = first.add_delta(jnp.concatenate([base_query, base_keyval], axis=1))
    heads_out[...] = total.astype(jnp.bfloat16).reshape(heads_out.shape)
    heads_copies = swap(lambda step, peer: heads_out.at[peer], heads_in, heads_sems)
    late_loads[1].wait()
    second.send_ups(wide_up)
    heads_in[0] = heads_out[my_shard]
    cosine = jnp.concatenate([cosines[...], cosines[...]], axis=1)
    sine = jnp.concatenate([-sines[...], sines[...]], axis=1)

    def rotated(vector):
        half = HD // 2
        swapped = jnp.concatenate([vector[:, half:], vector[:, :half]], axis=1)
        return vector * cosine + swapped * sine

    query_cols = query_weight.shape[1]
    per_group = QH // KVH
    per_shard = query_cols // HD
    keyval_shard = keyval_weight.shape[1] // HD
    for step in range(1, tp_count):
        heads_copies[step].wait_recv()
    for shard in range(tp_count):
        slot = lax.rem(my_shard - shard + tp_count, tp_count)
        block = heads_in[slot].astype(jnp.float32)
        for head in range(per_shard):
            queries[:, shard * per_shard + head, :] = rotated(
                block[:, head * HD : (head + 1) * HD]
            )
        for head in range(keyval_shard):
            number = shard * keyval_shard + head
            start = query_cols + head * HD
            vector = block[:, start : start + HD]
            target, vector = (keys, rotated(vector)) if number < KVH else (values, vector)
            for copy_of in range(per_group):
                target[:, (number % KVH) * per_group + copy_of, :] = vector
    loads[5].wait()
    attend_rows(cache, lengths, queries, keys, values, mixed)
    for shard in range(tp_count):
        for head in range(per_shard):
            mixed_out[shard, :, head * HD : (head + 1) * HD] = mixed[
                :, shard * per_shard + head, :
            ].astype(jnp.bfloat16)
    mixed_copies = swap(lambda step, peer: mixed_out.at[peer], mixed_in, mixed_sems)
    mixed_in[0] = mixed_out[my_shard]
    att_rows = mixed_in.shape[1]
    for step in range(tp_count):
        if step:
            mixed_copies[step].wait_recv()
        attended[pl.ds(pl.multiple_of(sender(step) * att_rows, att_rows), att_rows), :] = mixed_in[
            step
        ]
    own = attended[...]
    second.send_rows(own)
    loads[6].wait()
    out_width = out.shape[1]

    def output_share(peer):
        return dot_f32(
            own, output_weight[:, pl.ds(pl.multiple_of(peer * out_width, out_width), out_width)]
        )

    def staged_share(step, peer):
        share_out[step] = output_share(peer).astype(jnp.bfloat16)
        return share_out.at[step]

    share_copies = swap(staged_share, share_in, share_sems, early)
    for step in late:
        staged_share(step, lax.rem(my_shard + step, tp_count))
    base = output_share(my_shard)
    late_loads[0].wait()
    second.sum_rank(down)
    share_copies.update(
        swap(lambda step, peer: share_out.at[step], share_in, share_sems, late)
    )
    second.send_delta((wide_up,))
    for step in range(1, tp_count):
        share_copies[step].wait_recv()
        base = base + share_in[step].astype(jnp.float32)
    out[...] = second.add_delta(base).astype(jnp.bfloat16)
    for copy in sent:
        copy.wait_send()
    first.finish()
    second.finish()


def turn_table(lengths):
    half_dim = HD // 2
    frequency = rope_theta ** (-(2.0 * jnp.arange(half_dim, dtype=jnp.float32)) / HD)
    angles = lengths.astype(jnp.float32)[:, None] * frequency
    return jnp.cos(angles), jnp.sin(angles)


VMEM_SPEC = pl.BlockSpec(memory_space=pltpu.VMEM)
SMEM_SPEC = pl.BlockSpec(memory_space=pltpu.SMEM)
HBM_SPEC = pl.BlockSpec(memory_space=pl.ANY)


def routed_device(
    tokens,
    norm_gain,
    query_weight,
    keyval_weight,
    output_weight,
    projection_down_weight,
    query_up_weight,
    keyval_up_weight,
    output_down_weight,
    output_up_weight,
    adapter_ids,
    adapter_slot,
    kv_cache,
    cache_len,
):
    owner_count = lax.axis_size("req")
    tp_count = lax.axis_size("tp")
    held_count, width, rank = projection_down_weight.shape
    rows = tokens.shape[0]
    cap = FETCH_OWN * rows // owner_count
    att_rows = kv_cache.shape[0]
    query_cols = query_weight.shape[1]
    head_cols = query_cols + keyval_weight.shape[1]
    out_cols = output_up_weight.shape[2]
    sems = pltpu.SemaphoreType.DMA
    vmem = pltpu.VMEM
    return pl.pallas_call(
        functools.partial(layer_kernel, owner_count, tp_count),
        out_shape=jax.ShapeDtypeStruct((rows, out_cols), jnp.bfloat16),
        in_specs=[VMEM_SPEC] * 6 + [SMEM_SPEC] + [HBM_SPEC] * 9,
        out_specs=VMEM_SPEC,
        scratch_shapes=round_scratch(owner_count, tp_count, cap, width, rank, head_cols)
        + round_scratch(owner_count, tp_count, cap, query_cols, rank, out_cols)
        + [
            vmem((owner_count, 2 * rank, out_cols // 2), jnp.bfloat16),
            vmem((owner_count, 2 * rank, out_cols // 2), jnp.bfloat16),
            sems((2, owner_count)),
            vmem((owner_count, cap, 2 * rank), jnp.bfloat16),
            vmem((owner_count, cap, 2 * rank), jnp.bfloat16),
            sems((2, owner_count)),
        ]
        + [
            vmem(query_weight.shape, jnp.bfloat16),
            vmem(keyval_weight.shape, jnp.bfloat16),
            vmem(output_weight.shape, jnp.bfloat16),
            vmem((held_count, rank, width), jnp.bfloat16),
            vmem(query_up_weight.shape, jnp.bfloat16),
            vmem(keyval_up_weight.shape, jnp.bfloat16),
            vmem(kv_cache.shape, jnp.bfloat16),
            sems((9,)),
            vmem((owner_count, rows), jnp.int32),
            vmem((owner_count, cap, 1), jnp.int32),
            vmem((owner_count, cap, rows), jnp.bfloat16),
            vmem((owner_count, rows, cap), jnp.bfloat16),
            vmem((tp_count, 8, rows), jnp.float32),
            sems((2, tp_count)),
            vmem((tp_count, rows, width), jnp.bfloat16),
            sems((2, tp_count)),
            vmem((tp_count, att_rows, head_cols), jnp.bfloat16),
            vmem((tp_count, att_rows, head_cols), jnp.bfloat16),
            sems((2, tp_count)),
            vmem((att_rows, QH, HD), jnp.float32),
            vmem((att_rows, QH, HD), jnp.float32),
            vmem((att_rows, QH, HD), jnp.float32),
            vmem((att_rows, QH, HD), jnp.float32),
            vmem((tp_count, att_rows, query_cols), jnp.bfloat16),
            vmem((tp_count, att_rows, query_cols), jnp.bfloat16),
            sems((2, tp_count)),
            vmem((rows, query_cols), jnp.bfloat16),
            vmem((tp_count, rows, out_cols), jnp.bfloat16),
            vmem((tp_count, rows, out_cols), jnp.bfloat16),
            sems((2, tp_count)),
        ],
        compiler_params=pltpu.CompilerParams(
            collective_id=1, has_side_effects=True, vmem_limit_bytes=VMEM_BYTES
        ),
    )(
        tokens,
        norm_gain,
        adapter_ids.reshape(owner_count, rows),
        adapter_slot[None, :],
        *turn_table(cache_len),
        cache_len,
        query_weight,
        keyval_weight,
        output_weight,
        jnp.swapaxes(projection_down_weight, 1, 2),
        query_up_weight,
        keyval_up_weight,
        jnp.swapaxes(output_down_weight, 1, 2),
        output_up_weight,
        kv_cache,
    )


def fits_kernels(mesh):
    tp_count, owner_count = mesh.shape["tp"], mesh.shape["req"]
    return (2 * KVH * HD // tp_count) % HD == 0 and tp_count <= KVH and owner_count % 2 == 0


def solution(mesh):
    in_specs = (
        P(("group", "req"), "tp"),
        P("tp"),
        P(None, "tp"),
        P(None, "tp"),
        P("tp", None),
        P(("group", "req"), "tp", None),
        P(("group", "req"), None, "tp"),
        P(("group", "req"), None, "tp"),
        P(("group", "req"), "tp", None),
        P(("group", "req"), None, "tp"),
        P("group"),
        P("group"),
        P(("group", "req", "tp"), None, None),
        P(("group", "req", "tp")),
    )
    out_specs = P(("group", "req"), "tp")
    return jax.shard_map(
        routed_device if fits_kernels(mesh) else per_device,
        mesh=mesh, in_specs=in_specs, out_specs=out_specs, check_vma=False
    )
```
